128 devices in a mesh: member: 4 (over y), space: 32 (over x, z, core).
Axes of the slice: x: 4, y: 4, z: 4, core: 2. Of those that a mesh axis runs over, the one named last changes fastest.
Arguments:
- prior_ensemble: bfloat16 [96, 12, 65536], P('member', None, 'space'), may hold values from -48 to 48, as said below
- measured_readings: float32 [384, 4, 128], P('space', 'member'), may hold values from -8 to 8
- measurement_error_spread: float32 [384, 4, 128], P('space', 'member'), may hold values from 307 to 30720, as said below
- mapping_submatrices: bfloat16 [384, 4, 2, 128, 128], P('space', 'member'), may hold values from -0.375 to 0.375
- submatrix_target_slots: int32 [384, 4, 2], P('space', 'member'), may hold values from 0 to 15
Outputs:
- analysis: bfloat16 [96, 12, 65536], P('member', None, 'space')
- weights: float32 [96, 96], replicated
The draws below stay inside these ranges and needn't reach their ends.
Inputs may be any that keep to these rules, and one draw needn't show every extreme that they name: `prior_ensemble`: observed model fields with neighbouring members correlated. `measurement_error_spread`: Positive. `submatrix_target_slots`: column blocks lie in the first 4 variables.
All inputs are finite; a program needn't handle non-finite values.
Results may differ from the reference program's by a relative error of at most 0.006.
Values may be sent and summed in bfloat16 or wider, within the bound.
No kernel may reach another device: no remote copies, remote signals or barrier semaphores. Data moves between devices by JAX's collectives and lax.ppermute only.
A program may use at most 64 MiB of HBM per device.

```python
import math
import jax
import jax.numpy as jnp
from jax import lax

K = 96
V = 12
VOBS = 4
PATCH_GRIDPOINTS = 512
OBLK = 12
NNZ = 2
NS_ITERS = 4
CELLS = 65536
OBS = 196608
N_MEMBER = 4
N_SPACE = 32


def draw_prior_ensemble(key, part):
    key = jax.random.fold_in(key, 11)
    key_noise, key_base, key_scale = jax.random.split(key, 3)
    noise = jax.random.normal(key_noise, (K, V, CELLS), jnp.float32)
    mixing = 0.8
    correlated = noise + mixing * jnp.roll(noise, 1, axis=0)
    base_field = jax.random.normal(key_base, (1, V, CELLS), jnp.float32)
    scales = jnp.exp(jax.random.uniform(key_scale, (1, V, 1), jnp.float32, math.log(0.5), math.log(2.0)))
    return jnp.clip(base_field + correlated * scales, -48.0, 48.0).astype(jnp.bfloat16)


def draw_measurement_error_spread(key, part):
    key = jax.random.fold_in(key, 23)
    layout = (OBLK * N_SPACE, N_MEMBER, 128)
    spread_log = jax.random.uniform(key, layout, jnp.float32, math.log(0.3), math.log(3.0))
    block_rows = lax.broadcasted_iota(jnp.int32, layout, 0) // OBLK
    sub_tiles = lax.broadcasted_iota(jnp.int32, layout, 1)
    position = (block_rows * N_MEMBER + sub_tiles).astype(jnp.float32) / max(N_MEMBER * N_SPACE - 1, 1)
    return OBS / 64.0 * jnp.exp(spread_log) / jnp.power(3.0, position)


def with_ends(values, rng, least, top_value):
    shape = values.shape
    place = [jax.random.randint(jax.random.fold_in(rng, axis), (), 0, shape[axis]) for axis in range(len(shape))]
    values = values.at[tuple(place)].set(least)
    longest = shape.index(max(shape))
    place[longest] = (place[longest] + 1) % shape[longest]
    return values.at[tuple(place)].set(top_value)


def level_of(key, extent, pieces, least, largest):
    factor_of, own = 1.0, jax.random.fold_in(key, 6)
    for dim, blocks in pieces:
        heights = jnp.exp(jax.random.uniform(jax.random.fold_in(own, dim), (blocks,), jnp.float32, least / len(pieces), largest / len(pieces)))
        factor_of = factor_of * jnp.repeat(heights, extent[dim] // blocks).reshape([-1 if axis == dim else 1 for axis in range(len(extent))])
    return factor_of


def scatter_about(key, shape, width, most, cuts=(), kind=jnp.bfloat16):
    drawn = jax.random.normal(key, shape, jnp.float32) * width
    if len(cuts) > 0:
        drawn = level_of(key, shape, cuts, -0.22, 0.18) * drawn
    return jnp.clip(drawn, min=-most, max=most).astype(kind)


def setup_inputs(seed: int = 0) -> dict:
    seeds = jax.random.split(jax.random.key(seed), 6)
    prior_ensemble = draw_prior_ensemble(jax.random.fold_in(seeds[5], 71), 0)
    measured_readings = scatter_about(seeds[1], (OBLK * N_SPACE, N_MEMBER, 128), 1.5, 8.0, ((0, 32), (1, 4)), jnp.float32)
    measurement_error_spread = draw_measurement_error_spread(jax.random.fold_in(seeds[5], 71), 0)
    mapping_submatrices = scatter_about(seeds[3], (OBLK * N_SPACE, N_MEMBER, NNZ, 128, 128), (NNZ * 128) ** -0.5, 0.375, ((0, 32), (1, 4)))
    submatrix_target_slots = with_ends(jax.random.randint(seeds[4], (OBLK * N_SPACE, N_MEMBER, NNZ), 0, VOBS * PATCH_GRIDPOINTS // 128), jax.random.fold_in(seeds[4], 1), 0, (VOBS * PATCH_GRIDPOINTS // 128) - 1).astype(jnp.int32)
    return dict(prior_ensemble=prior_ensemble, measured_readings=measured_readings, measurement_error_spread=measurement_error_spread, mapping_submatrices=mapping_submatrices, submatrix_target_slots=submatrix_target_slots)


HIGHEST_MODE = lax.Precision.HIGHEST

def tile_order(values):
    rest_dims = values.shape[2:]
    grouped = values.reshape((N_SPACE, OBLK, N_MEMBER) + rest_dims)
    grouped = jnp.moveaxis(grouped, 2, 1)
    return grouped.reshape((N_SPACE * N_MEMBER, OBLK) + rest_dims)

def observe(state_piece, op_piece, col_piece):
    realisation_sequence = state_piece.shape[0]
    observed = state_piece[:, :VOBS].reshape(realisation_sequence, VOBS * PATCH_GRIDPOINTS // 128, 128)
    picked_rows = jnp.take(observed, col_piece.reshape(-1), axis=1)
    picked_rows = picked_rows.reshape(realisation_sequence, OBLK, NNZ, 128)
    return jnp.einsum('kbjc,bjoc->kbo', picked_rows.astype(jnp.float32), op_piece.astype(jnp.float32), precision=HIGHEST_MODE)

def ensemble_weights(gram, projected, realisation_sequence):
    eye_matrix = jnp.eye(realisation_sequence, dtype=jnp.float32)
    system = gram + (realisation_sequence - 1.0) * eye_matrix
    frob = jnp.sqrt(jnp.sum(system * system))

    def newton_step(step_index, carry):
        root_part, inverse_part = carry
        factor = 1.5 * eye_matrix - 0.5 * jnp.dot(inverse_part, root_part, precision=HIGHEST_MODE)
        return (jnp.dot(root_part, factor, precision=HIGHEST_MODE), jnp.dot(factor, inverse_part, precision=HIGHEST_MODE))
    root_part, inverse_part = lax.fori_loop(0, NS_ITERS, newton_step, (system / frob, eye_matrix))
    inverse_root = inverse_part / jnp.sqrt(frob)
    covariance = jnp.dot(inverse_root, inverse_root, precision=HIGHEST_MODE)
    mean_shift = jnp.dot(covariance, projected, precision=HIGHEST_MODE)
    return mean_shift[:, None] + jnp.sqrt(realisation_sequence - 1.0) * inverse_root

def reference(prior_ensemble, measured_readings, measurement_error_spread, mapping_submatrices, submatrix_target_slots):
    realisation_sequence = prior_ensemble.shape[0]
    tiles = N_MEMBER * N_SPACE
    op_tiles = tile_order(mapping_submatrices)
    col_tiles = tile_order(submatrix_target_slots)
    values = tile_order(measured_readings)
    variances = tile_order(measurement_error_spread)
    indices = jnp.arange(tiles, dtype=jnp.int32)

    def state_of(position_number):
        return lax.dynamic_slice_in_dim(prior_ensemble, (position_number * PATCH_GRIDPOINTS).astype(jnp.int32), PATCH_GRIDPOINTS, 2)

    def predict_tile(position_number):
        return observe(state_of(position_number), op_tiles[position_number], col_tiles[position_number])
    predicted = lax.map(predict_tile, indices)
    pred_mean = lax.optimization_barrier(jnp.mean(predicted, axis=1))
    spread = predicted - pred_mean[:, None]
    scaled = spread / variances[:, None]
    gram = jnp.einsum('tkbo,tlbo->kl', scaled, spread, precision=HIGHEST_MODE)
    projected = jnp.einsum('tkbo,tbo->k', scaled, values - pred_mean, precision=HIGHEST_MODE)
    weights = ensemble_weights(gram, projected, realisation_sequence)
    coeffs = weights.astype(jnp.bfloat16)
    keep = 1.0 - lax.optimization_barrier(jnp.sum(coeffs.astype(jnp.float32), axis=0))

    def analyse_tile(position_number):
        flat = state_of(position_number).reshape(realisation_sequence, V * PATCH_GRIDPOINTS)
        center = lax.optimization_barrier(jnp.sum(flat.astype(jnp.float32), axis=0)) / realisation_sequence
        mixed = jnp.dot(coeffs.T, flat, preferred_element_type=jnp.float32) + keep[:, None] * center[None, :]
        return mixed.astype(jnp.bfloat16).reshape(realisation_sequence, V, PATCH_GRIDPOINTS)
    analysed = lax.map(analyse_tile, indices)
    analysis = jnp.moveaxis(analysed, 0, 2).reshape(realisation_sequence, V, tiles * PATCH_GRIDPOINTS)
    return (analysis, weights)
```

```python
import jax
import jax.numpy as jnp
from jax import lax
from jax.experimental import pallas as pl
from jax.experimental.pallas import tpu as pltpu
from jax.sharding import PartitionSpec as P

K = 96
V = 12
VOBS = 4
MEMBERS = 24
GROUPS = 4
TILE = 512
BLOCKS = 12
NNZ = 2
NS_ITERS = 4

EXACT = lax.Precision.HIGHEST
VMEM = pl.BlockSpec(memory_space=pltpu.VMEM)
SMEM = pl.BlockSpec(memory_space=pltpu.SMEM)
ANY = pl.BlockSpec(memory_space=pl.ANY)
ROOM = pltpu.CompilerParams(vmem_limit_bytes=48 * 1024 * 1024)


def group_from(me, shift):
    return lax.rem(me + GROUPS - shift, GROUPS)


def group_to(me, shift):
    return lax.rem(me + shift, GROUPS)


def pack_kernel(me_ref, prior_ref, *refs):
    outs, sems = refs[:-1], refs[-1]
    me = me_ref[0]
    copies = []
    for s in range(GROUPS):
        cells = pl.ds(pl.multiple_of(group_to(me, s) * TILE, TILE), TILE)
        for part, rows in enumerate((pl.ds(0, VOBS), pl.ds(VOBS, V - VOBS))):
            n = part * GROUPS + s
            copies.append(
                pltpu.make_async_copy(prior_ref.at[rows, :, cells], outs[n], sems.at[n])
            )
    for copy in copies:
        copy.start()
    for copy in copies:
        copy.wait()


def pack(me, prior):
    shapes = [jax.ShapeDtypeStruct((VOBS, MEMBERS, TILE), prior.dtype)] * GROUPS
    shapes += [jax.ShapeDtypeStruct((V - VOBS, MEMBERS, TILE), prior.dtype)] * GROUPS
    outs = pl.pallas_call(
        pack_kernel,
        out_shape=shapes,
        in_specs=[SMEM, ANY],
        out_specs=[ANY] * len(shapes),
        scratch_shapes=[pltpu.SemaphoreType.DMA((2 * GROUPS,))],
        name="pack",
    )(me, prior)
    return outs[:GROUPS], outs[GROUPS:]


def observe_kernel(me_ref, slots_ref, c0, c1, c2, c3, op_ref, y_ref, var_ref, out_ref, state, spread, scaled):
    me = me_ref[0]
    for s, chunk in enumerate((c0, c1, c2, c3)):
        rows = pl.ds(pl.multiple_of(group_from(me, s) * MEMBERS, 8), MEMBERS)
        for v in range(VOBS):
            for c in range(TILE // 128):
                state[v * (TILE // 128) + c, rows, :] = chunk[v, :, c * 128 : (c + 1) * 128].astype(jnp.float32)
    spread[K:, :] = jnp.zeros((128 - K, BLOCKS * 128), jnp.float32)
    for b in range(BLOCKS):
        pred = jnp.zeros((K, 128), jnp.float32)
        for j in range(NNZ):
            part = state[slots_ref[b * NNZ + j]].astype(jnp.bfloat16)
            pred += lax.dot_general(
                part, op_ref[b, j], (((1,), (1,)), ((), ())), preferred_element_type=jnp.float32
            )
        mean = jnp.sum(pred, axis=0, keepdims=True) * (1.0 / K)
        dev = pred - mean
        lanes = pl.ds(b * 128, 128)
        spread[:K, lanes] = dev
        spread[K : K + 1, lanes] = y_ref[b : b + 1, :] - mean
        scaled[:, lanes] = dev / var_ref[b : b + 1, :]
    out_ref[...] = lax.dot_general(
        scaled[...], spread[...], (((1,), (1,)), ((), ())), precision=EXACT, preferred_element_type=jnp.float32
    )


def observe(me, slots, chunks, op, values, variances):
    return pl.pallas_call(
        observe_kernel,
        out_shape=jax.ShapeDtypeStruct((K, 128), jnp.float32),
        in_specs=[SMEM, SMEM] + [VMEM] * 7,
        out_specs=VMEM,
        scratch_shapes=[
            pltpu.VMEM((VOBS * TILE // 128, K, 128), jnp.float32),
            pltpu.VMEM((128, BLOCKS * 128), jnp.float32),
            pltpu.VMEM((K, BLOCKS * 128), jnp.float32),
        ],
        compiler_params=ROOM,
        name="observe",
    )(me, slots, *chunks, op, values, variances)


def exact_dot(a, b):
    return jnp.dot(a, b, precision=EXACT, preferred_element_type=jnp.float32)


def weights_kernel(sums_ref, weights_ref):
    sums = sums_ref[...]
    row = lax.broadcasted_iota(jnp.int32, (K, K), 0)
    col = lax.broadcasted_iota(jnp.int32, (K, K), 1)
    eye = jnp.where(row == col, 1.0, 0.0).astype(jnp.float32)
    system = sums[:, :K] + (K - 1.0) * eye
    projected = sums[:, K : K + 1]
    frob = jnp.sqrt(jnp.sum(system * system, keepdims=True))
    root = system / frob
    inverse = None
    for step in range(NS_ITERS):
        product = root if inverse is None else exact_dot(inverse, root)
        factor = 1.5 * eye - 0.5 * product
        if step < NS_ITERS - 1:
            root = exact_dot(root, factor)
        inverse = factor if inverse is None else exact_dot(factor, inverse)
    inverse_root = inverse / jnp.sqrt(frob)
    covariance = exact_dot(inverse_root, inverse_root)
    mean_shift = exact_dot(covariance, projected)
    weights_ref[...] = mean_shift + (K - 1.0) ** 0.5 * inverse_root


def make_weights(sums):
    return pl.pallas_call(
        weights_kernel,
        out_shape=jax.ShapeDtypeStruct((K, K), jnp.float32),
        in_specs=[VMEM],
        out_specs=VMEM,
        name="transform",
    )(sums)


def analyse_kernel(me_ref, w_ref, o0, o1, o2, o3, r0, r1, r2, r3, a0, a1, a2, a3, turned):
    me = me_ref[0]

    def regroup(x, which):
        return jnp.concatenate(
            [x[pl.ds(pl.multiple_of(which(me, s) * MEMBERS, 8), MEMBERS), :] for s in range(GROUPS)], axis=0
        )

    by_source = regroup(w_ref, group_from)
    turned[...] = by_source.T
    coeffs = regroup(turned, group_to).astype(jnp.bfloat16)
    keep = 1.0 - jnp.sum(coeffs.astype(jnp.float32), axis=1, keepdims=True)
    outs = (a0, a1, a2, a3)
    for v in range(V):
        src = (o0, o1, o2, o3) if v < VOBS else (r0, r1, r2, r3)
        u = v if v < VOBS else v - VOBS
        parts = [ref[u].astype(jnp.float32) for ref in src]
        stacked = jnp.concatenate(parts, axis=0)
        center = jnp.sum(stacked, axis=0, keepdims=True) * (1.0 / K)
        mixed = jnp.dot(coeffs, stacked.astype(jnp.bfloat16), preferred_element_type=jnp.float32)
        mixed = mixed + keep * center
        for g in range(GROUPS):
            outs[g][v] = mixed[g * MEMBERS : (g + 1) * MEMBERS].astype(jnp.bfloat16)


def analyse(me, weights, observed, rest):
    return pl.pallas_call(
        analyse_kernel,
        out_shape=[jax.ShapeDtypeStruct((V, MEMBERS, TILE), jnp.bfloat16)] * GROUPS,
        in_specs=[SMEM] + [VMEM] * 9,
        out_specs=[VMEM] * GROUPS,
        scratch_shapes=[pltpu.VMEM((K, K), jnp.float32)],
        compiler_params=ROOM,
        name="analyse",
    )(me, weights, *observed, *rest)


def place_kernel(me_ref, c0, c1, c2, c3, out_ref, sems):
    me = me_ref[0]
    copies = []
    for s, chunk in enumerate((c0, c1, c2, c3)):
        cells = pl.ds(pl.multiple_of(group_from(me, s) * TILE, TILE), TILE)
        copies.append(pltpu.make_async_copy(chunk, out_ref.at[:, :, cells], sems.at[s]))
    for copy in copies:
        copy.start()
    for copy in copies:
        copy.wait()


def place(me, chunks):
    return pl.pallas_call(
        place_kernel,
        out_shape=jax.ShapeDtypeStruct((V, MEMBERS, GROUPS * TILE), jnp.bfloat16),
        in_specs=[SMEM] + [ANY] * GROUPS,
        out_specs=ANY,
        scratch_shapes=[pltpu.SemaphoreType.DMA((GROUPS,))],
        name="place",
    )(me, *chunks)


def ring(shift):
    return [(i, (i + shift) % GROUPS) for i in range(GROUPS)]


def space_shift(dx, dz, dc):
    pairs = []
    for x in range(4):
        for z in range(4):
            for c in range(2):
                to = ((x + dx) % 4) * 8 + ((z + dz) % 4) * 2 + (c + dc) % 2
                pairs.append((x * 8 + z * 2 + c, to))
    return pairs


def scatter(chunks):
    return [chunks[0]] + [lax.ppermute(chunks[s], "member", ring(s)) for s in range(1, GROUPS)]


def total(x):
    x = x + lax.ppermute(x, "space", space_shift(0, 0, 1))
    parts = [lax.ppermute(x, "member", ring(s)) for s in (2, 1, 3)]
    x = (x + parts[0]) + (parts[1] + parts[2])
    parts = [lax.ppermute(x, "space", space_shift(0, s, 0)) for s in (2, 1, 3)]
    x = (x + parts[0]) + (parts[1] + parts[2])
    parts = [lax.ppermute(x, "space", space_shift(s, 0, 0)) for s in (2, 1, 3)]
    return (x + parts[0]) + (parts[1] + parts[2])


def body(prior, readings, error_spread, mapping, slots):
    me = lax.axis_index("member").astype(jnp.int32).reshape(1)
    observed_out, rest_out = pack(me, jnp.transpose(prior, (1, 0, 2)))
    observed = scatter(observed_out)
    rest = scatter(rest_out)
    sums = total(
        observe(me, slots.reshape(-1), observed, mapping[:, 0], readings[:, 0], error_spread[:, 0])
    )
    weights = make_weights(sums)
    chunks = analyse(me, weights, observed, rest)
    out = place(me, scatter(chunks))
    return (jnp.transpose(out, (1, 0, 2)), weights)


def solution(mesh):
    in_specs = (
        P("member", None, "space"),
        P("space", "member", None),
        P("space", "member", None),
        P("space", "member", None, None, None),
        P("space", "member", None),
    )
    out_specs = (P("member", None, "space"), P())
    return jax.shard_map(body, mesh=mesh, in_specs=in_specs, out_specs=out_specs, check_vma=False)
```

```python
import jax
import jax.numpy as jnp
from jax import lax
from jax.experimental import pallas as pl
from jax.experimental.pallas import tpu as pltpu
from jax.sharding import Mesh
from jax.sharding import PartitionSpec as P

K = 96
V = 12
VOBS = 4
MEMBERS = 24
GROUPS = 4
TILE = 512
BLOCKS = 12
NNZ = 2
NS_ITERS = 4
HALF = K // 2
CHIPS = 64

EXACT = lax.Precision.HIGHEST
VMEM = pl.BlockSpec(memory_space=pltpu.VMEM)
SMEM = pl.BlockSpec(memory_space=pltpu.SMEM)
ANY = pl.BlockSpec(memory_space=pl.ANY)
ROOM = pltpu.CompilerParams(vmem_limit_bytes=48 * 1024 * 1024)


def group_from(me, shift):
    return lax.rem(me + GROUPS - shift, GROUPS)


def group_to(me, shift):
    return lax.rem(me + shift, GROUPS)


def pack_kernel(me_ref, prior_ref, *refs):
    outs, sems = refs[:-1], refs[-1]
    me = me_ref[0]
    copies = []
    for s in range(GROUPS):
        cells = pl.ds(pl.multiple_of(group_to(me, s) * TILE, TILE), TILE)
        for part, rows in enumerate((pl.ds(0, VOBS), pl.ds(VOBS, V - VOBS))):
            n = part * GROUPS + s
            copies.append(
                pltpu.make_async_copy(prior_ref.at[rows, :, cells], outs[n], sems.at[n])
            )
    for copy in copies:
        copy.start()
    for copy in copies:
        copy.wait()


def pack(me, prior):
    shapes = [jax.ShapeDtypeStruct((VOBS, MEMBERS, TILE), prior.dtype)] * GROUPS
    shapes += [jax.ShapeDtypeStruct((V - VOBS, MEMBERS, TILE), prior.dtype)] * GROUPS
    outs = pl.pallas_call(
        pack_kernel,
        out_shape=shapes,
        in_specs=[SMEM, ANY],
        out_specs=[VMEM] * len(shapes),
        scratch_shapes=[pltpu.SemaphoreType.DMA((2 * GROUPS,))],
        name="pack",
    )(me, prior)
    return outs[:GROUPS], outs[GROUPS:]


def indices():
    row = lax.broadcasted_iota(jnp.int32, (HALF, 128), 0)
    lane = lax.broadcasted_iota(jnp.int32, (HALF, 128), 1)
    return row, lane


def fold(gram):
    row, lane = indices()
    top, low = gram[:HALF], gram[HALF:]
    second = pltpu.roll(low, 128 - HALF, 1)
    diagonal = jnp.sum(jnp.where(lane == row, second, 0.0), axis=1, keepdims=True)
    tail = jnp.sum(jnp.where(lane == HALF, second, 0.0), axis=1, keepdims=True)
    out = jnp.where((lane < HALF) & (lane > row), second, top)
    out = jnp.where(lane == K + 1, tail, out)
    return jnp.where(lane == K + 2, diagonal, out)


def unfold(folded):
    row, lane = indices()
    turned = jnp.concatenate([folded, jnp.zeros((128 - HALF, 128), jnp.float32)], axis=0).T
    flipped = turned[:HALF]
    first = jnp.where(lane <= row, folded, flipped)
    diagonal = folded[:, K + 2 : K + 3]
    second = jnp.where(lane < row, flipped, jnp.where(lane == row, diagonal, folded))
    top = jnp.where(lane < HALF, first, folded)
    low = jnp.where(lane < HALF, turned[HALF:K], pltpu.roll(second, HALF, 1))
    gram = jnp.concatenate([top, low], axis=0)[:, :K]
    projected = jnp.concatenate([folded[:, K : K + 1], folded[:, K + 1 : K + 2]], axis=0)
    return gram, projected


def observe_kernel(me_ref, slots_ref, c0, c1, c2, c3, op_ref, y_ref, var_ref, out_ref, state, spread, scaled):
    me = me_ref[0]
    for s, chunk in enumerate((c0, c1, c2, c3)):
        rows = pl.ds(pl.multiple_of(group_from(me, s) * MEMBERS, 8), MEMBERS)
        for v in range(VOBS):
            for c in range(TILE // 128):
                state[v * (TILE // 128) + c, rows, :] = chunk[v, :, c * 128 : (c + 1) * 128].astype(jnp.float32)
    spread[K:, :] = jnp.zeros((128 - K, BLOCKS * 128), jnp.float32)
    for b in range(BLOCKS):
        pred = jnp.zeros((K, 128), jnp.float32)
        for j in range(NNZ):
            part = state[slots_ref[b * NNZ + j]].astype(jnp.bfloat16)
            pred += lax.dot_general(
                part, op_ref[b, j], (((1,), (1,)), ((), ())), preferred_element_type=jnp.float32
            )
        mean = jnp.sum(pred, axis=0, keepdims=True) * (1.0 / K)
        dev = pred - mean
        lanes = pl.ds(b * 128, 128)
        spread[:K, lanes] = dev
        spread[K : K + 1, lanes] = y_ref[b : b + 1, :] - mean
        scaled[:, lanes] = dev / var_ref[b : b + 1, :]
    gram = lax.dot_general(
        scaled[...], spread[...], (((1,), (1,)), ((), ())), precision=EXACT, preferred_element_type=jnp.float32
    )
    out_ref[...] = fold(gram)


def observe(me, slots, chunks, op, values, variances):
    return pl.pallas_call(
        observe_kernel,
        out_shape=jax.ShapeDtypeStruct((HALF, 128), jnp.float32),
        in_specs=[SMEM, SMEM] + [VMEM] * 7,
        out_specs=VMEM,
        scratch_shapes=[
            pltpu.VMEM((VOBS * TILE // 128, K, 128), jnp.float32),
            pltpu.VMEM((128, BLOCKS * 128), jnp.float32),
            pltpu.VMEM((K, BLOCKS * 128), jnp.float32),
        ],
        compiler_params=ROOM,
        name="observe",
    )(me, slots, *chunks, op, values, variances)


def split(a):
    high = a.astype(jnp.bfloat16)
    return high, (a - high.astype(jnp.float32)).astype(jnp.bfloat16)


def fine_dot(a, b):
    a_high, a_low = split(a)
    b_high, b_low = split(b)
    small = jnp.dot(a_high, b_low, preferred_element_type=jnp.float32)
    small += jnp.dot(a_low, b_high, preferred_element_type=jnp.float32)
    return small + jnp.dot(a_high, b_high, preferred_element_type=jnp.float32)


def transform_kernel(core_ref, mine_ref, other_ref, weights_ref):
    first = core_ref[0] == 0
    mine, other = mine_ref[...], other_ref[...]
    folded = jnp.concatenate([jnp.where(first, mine, other), jnp.where(first, other, mine)], axis=0)
    gram, projected = unfold(folded)
    row = lax.broadcasted_iota(jnp.int32, (K, K), 0)
    col = lax.broadcasted_iota(jnp.int32, (K, K), 1)
    eye = jnp.where(row == col, 1.0, 0.0).astype(jnp.float32)
    system = gram + (K - 1.0) * eye
    frob = jnp.sqrt(jnp.sum(system * system, keepdims=True))
    root = system / frob
    inverse = None
    for step in range(NS_ITERS):
        product = root if inverse is None else fine_dot(inverse, root)
        factor = 1.5 * eye - 0.5 * product
        if step < NS_ITERS - 1:
            root = fine_dot(root, factor)
        inverse = factor if inverse is None else fine_dot(factor, inverse)
    inverse_root = inverse / jnp.sqrt(frob)
    halfway = jnp.sum(inverse_root * projected, axis=0, keepdims=True)
    mean_shift = jnp.sum(inverse_root * halfway, axis=1, keepdims=True)
    weights_ref[...] = mean_shift + (K - 1.0) ** 0.5 * inverse_root


def transform(core, mine, other):
    return pl.pallas_call(
        transform_kernel,
        out_shape=jax.ShapeDtypeStruct((K, K), jnp.float32),
        in_specs=[SMEM, VMEM, VMEM],
        out_specs=VMEM,
        name="transform",
    )(core, mine, other)


def analyse_kernel(me_ref, w_ref, o0, o1, o2, o3, r0, r1, r2, r3, a0, a1, a2, a3, turned):
    me = me_ref[0]

    def regroup(x, which):
        return jnp.concatenate(
            [x[pl.ds(pl.multiple_of(which(me, s) * MEMBERS, 8), MEMBERS), :] for s in range(GROUPS)], axis=0
        )

    by_source = regroup(w_ref, group_from)
    turned[...] = by_source.T
    coeffs = regroup(turned, group_to).astype(jnp.bfloat16)
    keep = 1.0 - jnp.sum(coeffs.astype(jnp.float32), axis=1, keepdims=True)
    outs = (a0, a1, a2, a3)
    for v in range(V):
        src = (o0, o1, o2, o3) if v < VOBS else (r0, r1, r2, r3)
        u = v if v < VOBS else v - VOBS
        parts = [ref[u].astype(jnp.float32) for ref in src]
        stacked = jnp.concatenate(parts, axis=0)
        center = jnp.sum(stacked, axis=0, keepdims=True) * (1.0 / K)
        mixed = jnp.dot(coeffs, stacked.astype(jnp.bfloat16), preferred_element_type=jnp.float32)
        mixed = mixed + keep * center
        for g in range(GROUPS):
            outs[g][v] = mixed[g * MEMBERS : (g + 1) * MEMBERS].astype(jnp.bfloat16)


def analyse(me, weights, observed, rest):
    return pl.pallas_call(
        analyse_kernel,
        out_shape=[jax.ShapeDtypeStruct((V, MEMBERS, TILE), jnp.bfloat16)] * GROUPS,
        in_specs=[SMEM] + [VMEM] * 9,
        out_specs=[VMEM] * GROUPS,
        scratch_shapes=[pltpu.VMEM((K, K), jnp.float32)],
        compiler_params=ROOM,
        name="analyse",
    )(me, weights, *observed, *rest)


def place_kernel(me_ref, c0, c1, c2, c3, out_ref, sems):
    me = me_ref[0]
    copies = []
    for s, chunk in enumerate((c0, c1, c2, c3)):
        cells = pl.ds(pl.multiple_of(group_from(me, s) * TILE, TILE), TILE)
        copies.append(pltpu.make_async_copy(chunk, out_ref.at[:, :, cells], sems.at[s]))
    for copy in copies:
        copy.start()
    for copy in copies:
        copy.wait()


def place(me, chunks):
    return pl.pallas_call(
        place_kernel,
        out_shape=jax.ShapeDtypeStruct((V, MEMBERS, GROUPS * TILE), jnp.bfloat16),
        in_specs=[SMEM] + [VMEM] * GROUPS,
        out_specs=ANY,
        scratch_shapes=[pltpu.SemaphoreType.DMA((GROUPS,))],
        name="place",
    )(me, *chunks)


def ring(shift):
    return [(i, (i + shift) % GROUPS) for i in range(GROUPS)]


def scatter(chunks):
    return [chunks[0]] + [lax.ppermute(chunks[s], "member", ring(s)) for s in range(1, GROUPS)]


def swap(x):
    return lax.ppermute(x, "core", [(0, 1), (1, 0)])


def total(core, folded):
    first = core[0] == 0
    top, low = folded[: HALF // 2], folded[HALF // 2 :]
    chip = jnp.where(first, top, low) + swap(jnp.where(first, low, top))
    copies = jnp.broadcast_to(chip[None], (CHIPS, HALF // 2, 128))
    mine = jnp.sum(lax.all_to_all(copies, ("member", "x", "z"), 0, 0, tiled=True), axis=0)
    return mine, swap(mine)


def body(prior, readings, error_spread, mapping, slots):
    me = lax.axis_index("member").astype(jnp.int32).reshape(1)
    core = lax.axis_index("core").astype(jnp.int32).reshape(1)
    observed_out, rest_out = pack(me, jnp.transpose(prior, (1, 0, 2)))
    observed = scatter(observed_out)
    rest = scatter(rest_out)
    folded = observe(me, slots.reshape(-1), observed, mapping[:, 0], readings[:, 0], error_spread[:, 0])
    weights = transform(core, *total(core, folded))
    out = place(me, scatter(analyse(me, weights, observed, rest)))
    return (jnp.transpose(out, (1, 0, 2)), weights)


def solution(mesh):
    devices = mesh.devices.reshape(GROUPS, 4, 4, 2)
    axes = Mesh(devices, ("member", "x", "z", "core"))
    space = ("x", "z", "core")
    in_specs = (
        P("member", None, space),
        P(space, "member", None),
        P(space, "member", None),
        P(space, "member", None, None, None),
        P(space, "member", None),
    )
    out_specs = (P("member", None, space), P())
    return jax.shard_map(body, mesh=axes, in_specs=in_specs, out_specs=out_specs, check_vma=False)
```

```python
import functools

import jax
import jax.numpy as jnp
from jax import lax
from jax.experimental import pallas as pl
from jax.experimental.pallas import tpu as pltpu
from jax.sharding import Mesh
from jax.sharding import PartitionSpec as P

K = 96
V = 12
VOBS = 4
MEMBERS = 24
GROUPS = 4
TILE = 512
BLOCKS = 12
NNZ = 2
NS_ITERS = 4
HALF = K // 2
PLANE = 16

EXACT = lax.Precision.HIGHEST
VMEM = pl.BlockSpec(memory_space=pltpu.VMEM)
SMEM = pl.BlockSpec(memory_space=pltpu.SMEM)
ANY = pl.BlockSpec(memory_space=pl.ANY)
ROOM = pltpu.CompilerParams(vmem_limit_bytes=8 * 1024 * 1024)


def group_from(me, shift):
    return lax.rem(me + GROUPS - shift, GROUPS)


def group_to(me, shift):
    return lax.rem(me + shift, GROUPS)


def pack_kernel(me_ref, prior_ref, *refs):
    outs, sems = refs[:-1], refs[-1]
    me = me_ref[0]
    copies = []
    for s in range(GROUPS):
        cells = pl.ds(pl.multiple_of(group_to(me, s) * TILE, TILE), TILE)
        for part, rows in enumerate((pl.ds(0, VOBS), pl.ds(VOBS, V - VOBS))):
            n = part * GROUPS + s
            copies.append(
                pltpu.make_async_copy(prior_ref.at[rows, :, cells], outs[n], sems.at[n])
            )
    for copy in copies:
        copy.start()
    for copy in copies:
        copy.wait()


def pack(me, prior):
    shapes = [jax.ShapeDtypeStruct((VOBS, MEMBERS, TILE), prior.dtype)] * GROUPS
    shapes += [jax.ShapeDtypeStruct((V - VOBS, MEMBERS, TILE), prior.dtype)] * GROUPS
    outs = pl.pallas_call(
        pack_kernel,
        out_shape=shapes,
        in_specs=[SMEM, ANY],
        out_specs=[VMEM] * len(shapes),
        scratch_shapes=[pltpu.SemaphoreType.DMA((2 * GROUPS,))],
        compiler_params=ROOM,
        name="pack",
    )(me, prior)
    return outs[:GROUPS], outs[GROUPS:]


def indices():
    row = lax.broadcasted_iota(jnp.int32, (HALF, 128), 0)
    lane = lax.broadcasted_iota(jnp.int32, (HALF, 128), 1)
    return row, lane


def fold(gram):
    row, lane = indices()
    top, low = gram[:HALF], gram[HALF:]
    second = pltpu.roll(low, 128 - HALF, 1)
    diagonal = jnp.sum(jnp.where(lane == row, second, 0.0), axis=1, keepdims=True)
    tail = jnp.sum(jnp.where(lane == HALF, second, 0.0), axis=1, keepdims=True)
    out = jnp.where((lane < HALF) & (lane > row), second, top)
    out = jnp.where(lane == K + 1, tail, out)
    return jnp.where(lane == K + 2, diagonal, out)


def unfold(folded):
    row, lane = indices()
    turned = jnp.concatenate([folded, jnp.zeros((128 - HALF, 128), jnp.float32)], axis=0).T
    flipped = turned[:HALF]
    first = jnp.where(lane <= row, folded, flipped)
    diagonal = folded[:, K + 2 : K + 3]
    second = jnp.where(lane < row, flipped, jnp.where(lane == row, diagonal, folded))
    top = jnp.where(lane < HALF, first, folded)
    low = jnp.where(lane < HALF, turned[HALF:K], pltpu.roll(second, HALF, 1))
    gram = jnp.concatenate([top, low], axis=0)[:, :K]
    projected = jnp.concatenate([folded[:, K : K + 1], folded[:, K + 1 : K + 2]], axis=0)
    return gram, projected


def observe_kernel(me_ref, slots_ref, c0, c1, c2, c3, op_ref, y_ref, var_ref, out_ref, state, spread, scaled):
    me = me_ref[0]
    for s, chunk in enumerate((c0, c1, c2, c3)):
        rows = pl.ds(pl.multiple_of(group_from(me, s) * MEMBERS, 8), MEMBERS)
        for v in range(VOBS):
            for c in range(TILE // 128):
                state[v * (TILE // 128) + c, rows, :] = chunk[v, :, c * 128 : (c + 1) * 128].astype(jnp.float32)
    spread[K:, :] = jnp.zeros((128 - K, BLOCKS * 128), jnp.float32)
    for b in range(BLOCKS):
        pred = jnp.zeros((K, 128), jnp.float32)
        for j in range(NNZ):
            part = state[slots_ref[b * NNZ + j]].astype(jnp.bfloat16)
            pred += lax.dot_general(
                part, op_ref[b, j], (((1,), (1,)), ((), ())), preferred_element_type=jnp.float32
            )
        mean = jnp.sum(pred, axis=0, keepdims=True) * (1.0 / K)
        dev = pred - mean
        lanes = pl.ds(b * 128, 128)
        spread[:K, lanes] = dev
        spread[K : K + 1, lanes] = y_ref[b : b + 1, :] - mean
        scaled[:, lanes] = dev / var_ref[b : b + 1, :]
    gram = lax.dot_general(
        scaled[...], spread[...], (((1,), (1,)), ((), ())), precision=EXACT, preferred_element_type=jnp.float32
    )
    out_ref[...] = fold(gram)


def observe(me, slots, chunks, op, values, variances):
    return pl.pallas_call(
        observe_kernel,
        out_shape=jax.ShapeDtypeStruct((HALF, 128), jnp.float32),
        in_specs=[SMEM, SMEM] + [VMEM] * 7,
        out_specs=VMEM,
        scratch_shapes=[
            pltpu.VMEM((VOBS * TILE // 128, K, 128), jnp.float32),
            pltpu.VMEM((128, BLOCKS * 128), jnp.float32),
            pltpu.VMEM((K, BLOCKS * 128), jnp.float32),
        ],
        compiler_params=ROOM,
        name="observe",
    )(me, slots, *chunks, op, values, variances)


def split(a):
    high = a.astype(jnp.bfloat16)
    return high, (a - high.astype(jnp.float32)).astype(jnp.bfloat16)


def fine_dot(a, b):
    a_high, a_low = split(a)
    b_high, b_low = split(b)
    small = jnp.dot(a_high, b_low, preferred_element_type=jnp.float32)
    small += jnp.dot(a_low, b_high, preferred_element_type=jnp.float32)
    return small + jnp.dot(a_high, b_high, preferred_element_type=jnp.float32)


def transform_kernel(core_ref, mine_ref, other_ref, weights_ref):
    first = core_ref[0] == 0
    mine, other = mine_ref[...], other_ref[...]
    folded = jnp.concatenate([jnp.where(first, mine, other), jnp.where(first, other, mine)], axis=0)
    gram, projected = unfold(folded)
    row = lax.broadcasted_iota(jnp.int32, (K, K), 0)
    col = lax.broadcasted_iota(jnp.int32, (K, K), 1)
    eye = jnp.where(row == col, 1.0, 0.0).astype(jnp.float32)
    system = gram + (K - 1.0) * eye
    frob = jnp.sqrt(jnp.sum(system * system, keepdims=True))
    root = system / frob
    inverse = None
    for step in range(NS_ITERS):
        product = root if inverse is None else fine_dot(inverse, root)
        factor = 1.5 * eye - 0.5 * product
        if step < NS_ITERS - 1:
            root = fine_dot(root, factor)
        inverse = factor if inverse is None else fine_dot(factor, inverse)
    inverse_root = inverse / jnp.sqrt(frob)
    halfway = jnp.sum(inverse_root * projected, axis=0, keepdims=True)
    mean_shift = jnp.sum(inverse_root * halfway, axis=1, keepdims=True)
    weights_ref[...] = mean_shift + (K - 1.0) ** 0.5 * inverse_root


def transform(core, mine, other):
    return pl.pallas_call(
        transform_kernel,
        out_shape=jax.ShapeDtypeStruct((K, K), jnp.float32),
        in_specs=[SMEM, VMEM, VMEM],
        out_specs=VMEM,
        compiler_params=ROOM,
        name="transform",
    )(core, mine, other)


def analyse_kernel(me_ref, w_ref, o0, o1, o2, o3, r0, r1, r2, r3, a0, a1, a2, a3, turned):
    me = me_ref[0]

    def regroup(x, which):
        return jnp.concatenate(
            [x[pl.ds(pl.multiple_of(which(me, s) * MEMBERS, 8), MEMBERS), :] for s in range(GROUPS)], axis=0
        )

    by_source = regroup(w_ref, group_from)
    turned[...] = by_source.T
    coeffs = regroup(turned, group_to).astype(jnp.bfloat16)
    keep = 1.0 - jnp.sum(coeffs.astype(jnp.float32), axis=1, keepdims=True)
    outs = (a0, a1, a2, a3)
    for v in range(V):
        src = (o0, o1, o2, o3) if v < VOBS else (r0, r1, r2, r3)
        u = v if v < VOBS else v - VOBS
        parts = [ref[u].astype(jnp.float32) for ref in src]
        stacked = jnp.concatenate(parts, axis=0)
        center = jnp.sum(stacked, axis=0, keepdims=True) * (1.0 / K)
        mixed = jnp.dot(coeffs, stacked.astype(jnp.bfloat16), preferred_element_type=jnp.float32)
        mixed = mixed + keep * center
        for g in range(GROUPS):
            outs[g][v] = mixed[g * MEMBERS : (g + 1) * MEMBERS].astype(jnp.bfloat16)


def analyse(me, weights, observed, rest):
    return pl.pallas_call(
        analyse_kernel,
        out_shape=[jax.ShapeDtypeStruct((V, MEMBERS, TILE), jnp.bfloat16)] * GROUPS,
        in_specs=[SMEM] + [VMEM] * 9,
        out_specs=[VMEM] * GROUPS,
        scratch_shapes=[pltpu.VMEM((K, K), jnp.float32)],
        compiler_params=ROOM,
        name="analyse",
    )(me, weights, *observed, *rest)


def place_kernel(shift, me_ref, chunk, *refs):
    out_ref, sem = refs[-2:]
    cells = pl.ds(pl.multiple_of(group_from(me_ref[0], shift) * TILE, TILE), TILE)
    copy = pltpu.make_async_copy(chunk, out_ref.at[:, :, cells], sem)
    copy.start()
    copy.wait()


def place(me, chunks):
    out = []
    for shift, chunk in enumerate(chunks):
        out = [
            pl.pallas_call(
                functools.partial(place_kernel, shift),
                out_shape=jax.ShapeDtypeStruct((V, MEMBERS, GROUPS * TILE), jnp.bfloat16),
                in_specs=[SMEM, VMEM] + [ANY] * len(out),
                out_specs=ANY,
                scratch_shapes=[pltpu.SemaphoreType.DMA],
                input_output_aliases={2: 0} if out else {},
                compiler_params=ROOM,
                name="place",
            )(me, chunk, *out)
        ]
    return out[0]


def ring(shift):
    return [(i, (i + shift) % GROUPS) for i in range(GROUPS)]


def scatter(chunks):
    return [chunks[0]] + [lax.ppermute(chunks[s], "member", ring(s)) for s in range(1, GROUPS)]


def swap(x):
    return lax.ppermute(x, "core", [(0, 1), (1, 0)])


def total(core, folded):
    first = core[0] == 0
    top, low = folded[: HALF // 2], folded[HALF // 2 :]
    chip = jnp.where(first, top, low) + swap(jnp.where(first, low, top))
    parts = [lax.ppermute(chip, "member", ring(s)) for s in (2, 1, 3)]
    chip = (chip + parts[0]) + (parts[1] + parts[2])
    copies = jnp.broadcast_to(chip[None], (PLANE, HALF // 2, 128))
    mine = jnp.sum(lax.all_to_all(copies, ("x", "z"), 0, 0, tiled=True), axis=0)
    return mine, swap(mine)


def body(prior, readings, error_spread, mapping, slots):
    me = lax.axis_index("member").astype(jnp.int32).reshape(1)
    core = lax.axis_index("core").astype(jnp.int32).reshape(1)
    observed_out, rest_out = pack(me, jnp.transpose(prior, (1, 0, 2)))
    observed = scatter(observed_out)
    rest = scatter(rest_out)
    folded = observe(me, slots.reshape(-1), observed, mapping[:, 0], readings[:, 0], error_spread[:, 0])
    weights = transform(core, *total(core, folded))
    out = place(me, scatter(analyse(me, weights, observed, rest)))
    return (jnp.transpose(out, (1, 0, 2)), weights)


def solution(mesh):
    devices = mesh.devices.reshape(GROUPS, 4, 4, 2)
    axes = Mesh(devices, ("member", "x", "z", "core"))
    space = ("x", "z", "core")
    in_specs = (
        P("member", None, space),
        P(space, "member", None),
        P(space, "member", None),
        P(space, "member", None, None, None),
        P(space, "member", None),
    )
    out_specs = (P("member", None, space), P())
    return jax.shard_map(body, mesh=axes, in_specs=in_specs, out_specs=out_specs, check_vma=False)
```

```python
import functools

import jax
import jax.numpy as jnp
from jax import lax
from jax.experimental import pallas as pl
from jax.experimental.pallas import tpu as pltpu
from jax.sharding import Mesh
from jax.sharding import PartitionSpec as P

K = 96
V = 12
VOBS = 4
MEMBERS = 24
GROUPS = 4
TILE = 512
BLOCKS = 12
NNZ = 2
NS_ITERS = 4
HALF = K // 2
PLANE = 16
COLUMN = 8
NEAR = 6
COST = 40_000_000_000
FAR = V - NEAR
NEXT = NEAR - VOBS

EXACT = lax.Precision.HIGHEST
VMEM = pl.BlockSpec(memory_space=pltpu.VMEM)
SMEM = pl.BlockSpec(memory_space=pltpu.SMEM)
HBM = pl.BlockSpec(memory_space=pltpu.HBM)
ANY = pl.BlockSpec(memory_space=pl.ANY)
ROOM = pltpu.CompilerParams(vmem_limit_bytes=8 * 1024 * 1024)


def group_from(me, shift):
    return lax.rem(me + GROUPS - shift, GROUPS)


def group_to(me, shift):
    return lax.rem(me + shift, GROUPS)


def pack_kernel(me_ref, prior_ref, *refs):
    outs, sems = refs[:-1], refs[-1]
    copies = []
    for s in range(GROUPS):
        cells = pl.ds(pl.multiple_of(group_to(me_ref[0], s) * TILE, TILE), TILE)
        copies.append(pltpu.make_async_copy(prior_ref.at[pl.ds(0, VOBS), :, cells], outs[s], sems.at[s]))
    for copy in copies:
        copy.start()
    for copy in copies:
        copy.wait()


def pack(me, prior):
    return pl.pallas_call(
        pack_kernel,
        out_shape=[jax.ShapeDtypeStruct((VOBS, MEMBERS, TILE), prior.dtype)] * GROUPS,
        in_specs=[SMEM, HBM],
        out_specs=[VMEM] * GROUPS,
        scratch_shapes=[pltpu.SemaphoreType.DMA((GROUPS,))],
        compiler_params=ROOM,
        name="pack",
    )(me, prior)


def pack_bulk_kernel(me_ref, prior_ref, after_ref, *refs):
    del after_ref
    outs, sems = refs[:-1], refs[-1]
    copies = []
    for s in range(GROUPS):
        cells = pl.ds(pl.multiple_of(group_to(me_ref[0], s) * TILE, TILE), TILE)
        if NEXT:
            copies.append((prior_ref.at[pl.ds(VOBS, NEXT), :, cells], outs[s].at[pl.ds(0, NEXT)]))
        for c in range(GROUPS):
            source = prior_ref.at[pl.ds(NEAR, FAR), :, pl.ds(c * TILE, TILE)]
            copies.append((source, outs[s].at[pl.ds(NEXT + c * FAR, FAR)]))
    copies = [pltpu.make_async_copy(*pair, sems.at[n]) for n, pair in enumerate(copies)]
    for copy in copies:
        copy.start()
    for copy in copies:
        copy.wait()


def pack_bulk(me, prior, after):
    return pl.pallas_call(
        pack_bulk_kernel,
        out_shape=[jax.ShapeDtypeStruct((NEXT + GROUPS * FAR, MEMBERS, TILE), prior.dtype)] * GROUPS,
        in_specs=[SMEM, ANY, ANY],
        out_specs=[VMEM] * GROUPS,
        scratch_shapes=[pltpu.SemaphoreType.DMA((GROUPS * (GROUPS + 1),))],
        compiler_params=ROOM,
        name="pack_bulk",
    )(me, prior, after)


def indices():
    row = lax.broadcasted_iota(jnp.int32, (HALF, 128), 0)
    lane = lax.broadcasted_iota(jnp.int32, (HALF, 128), 1)
    return row, lane


def fold(gram):
    row, lane = indices()
    top, low = gram[:HALF], gram[HALF:]
    second = pltpu.roll(low, 128 - HALF, 1)
    diagonal = jnp.sum(jnp.where(lane == row, second, 0.0), axis=1, keepdims=True)
    tail = jnp.sum(jnp.where(lane == HALF, second, 0.0), axis=1, keepdims=True)
    out = jnp.where((lane < HALF) & (lane > row), second, top)
    out = jnp.where(lane == K + 1, tail, out)
    return jnp.where(lane == K + 2, diagonal, out)


def unfold(folded):
    row, lane = indices()
    turned = jnp.concatenate([folded, jnp.zeros((128 - HALF, 128), jnp.float32)], axis=0).T
    flipped = turned[:HALF]
    first = jnp.where(lane <= row, folded, flipped)
    diagonal = folded[:, K + 2 : K + 3]
    second = jnp.where(lane < row, flipped, jnp.where(lane == row, diagonal, folded))
    top = jnp.where(lane < HALF, first, folded)
    low = jnp.where(lane < HALF, turned[HALF:K], pltpu.roll(second, HALF, 1))
    gram = jnp.concatenate([top, low], axis=0)[:, :K]
    projected = jnp.concatenate([folded[:, K : K + 1], folded[:, K + 1 : K + 2]], axis=0)
    return gram, projected


def observe_kernel(me_ref, slots_ref, c0, c1, c2, c3, op_ref, y_ref, var_ref, out_ref, state, spread, scaled):
    me = me_ref[0]
    for s, chunk in enumerate((c0, c1, c2, c3)):
        rows = pl.ds(pl.multiple_of(group_from(me, s) * MEMBERS, 8), MEMBERS)
        for v in range(VOBS):
            for c in range(TILE // 128):
                state[v * (TILE // 128) + c, rows, :] = chunk[v, :, c * 128 : (c + 1) * 128].astype(jnp.float32)
    spread[K:, :] = jnp.zeros((128 - K, BLOCKS * 128), jnp.float32)
    for b in range(BLOCKS):
        pred = jnp.zeros((K, 128), jnp.float32)
        for j in range(NNZ):
            part = state[slots_ref[b * NNZ + j]].astype(jnp.bfloat16)
            pred += lax.dot_general(
                part, op_ref[b, j], (((1,), (1,)), ((), ())), preferred_element_type=jnp.float32
            )
        mean = jnp.sum(pred, axis=0, keepdims=True) * (1.0 / K)
        dev = pred - mean
        lanes = pl.ds(b * 128, 128)
        spread[:K, lanes] = dev
        spread[K : K + 1, lanes] = y_ref[b : b + 1, :] - mean
        scaled[:, lanes] = dev / var_ref[b : b + 1, :]
    gram = lax.dot_general(
        scaled[...], spread[...], (((1,), (1,)), ((), ())), precision=EXACT, preferred_element_type=jnp.float32
    )
    out_ref[...] = fold(gram)


def observe(me, slots, chunks, op, values, variances):
    return pl.pallas_call(
        observe_kernel,
        out_shape=jax.ShapeDtypeStruct((HALF, 128), jnp.float32),
        in_specs=[SMEM, SMEM] + [VMEM] * 7,
        out_specs=VMEM,
        scratch_shapes=[
            pltpu.VMEM((VOBS * TILE // 128, K, 128), jnp.float32),
            pltpu.VMEM((128, BLOCKS * 128), jnp.float32),
            pltpu.VMEM((K, BLOCKS * 128), jnp.float32),
        ],
        compiler_params=ROOM,
        name="observe",
    )(me, slots, *chunks, op, values, variances)


def split(a):
    high = a.astype(jnp.bfloat16)
    return high, (a - high.astype(jnp.float32)).astype(jnp.bfloat16)


def fine_dot(a, b):
    a_high, a_low = split(a)
    b_high, b_low = split(b)
    small = jnp.dot(a_high, b_low, preferred_element_type=jnp.float32)
    small += jnp.dot(a_low, b_high, preferred_element_type=jnp.float32)
    return small + jnp.dot(a_high, b_high, preferred_element_type=jnp.float32)


def spread_kernel(parts_ref, out_ref):
    total = parts_ref[0]
    for part in range(1, parts_ref.shape[0]):
        total = total + parts_ref[part]
    for copy in range(out_ref.shape[0]):
        out_ref[copy] = total


def spread_sum(parts, copies):
    return pl.pallas_call(
        spread_kernel,
        out_shape=jax.ShapeDtypeStruct((copies, HALF, 128), jnp.float32),
        in_specs=[VMEM],
        out_specs=VMEM,
        compiler_params=ROOM,
        name="spread_sum",
    )(parts)


def transform_kernel(parts_ref, weights_ref, again_ref):
    folded = parts_ref[...]
    gram, projected = unfold(folded)
    row = lax.broadcasted_iota(jnp.int32, (K, K), 0)
    col = lax.broadcasted_iota(jnp.int32, (K, K), 1)
    eye = jnp.where(row == col, 1.0, 0.0).astype(jnp.float32)
    system = gram + (K - 1.0) * eye
    frob = jnp.sqrt(jnp.sum(system * system, keepdims=True))
    root = system / frob
    inverse = None
    for step in range(NS_ITERS):
        product = root if inverse is None else fine_dot(inverse, root)
        factor = 1.5 * eye - 0.5 * product
        if step < NS_ITERS - 1:
            root = fine_dot(root, factor)
        inverse = factor if inverse is None else fine_dot(factor, inverse)
    inverse_root = inverse / jnp.sqrt(frob)
    halfway = jnp.sum(inverse_root * projected, axis=0, keepdims=True)
    mean_shift = jnp.sum(inverse_root * halfway, axis=1, keepdims=True)
    weights = mean_shift + (K - 1.0) ** 0.5 * inverse_root
    weights_ref[...] = weights
    again_ref[...] = weights


def transform(parts):
    return pl.pallas_call(
        transform_kernel,
        out_shape=[jax.ShapeDtypeStruct((K, K), jnp.float32)] * 2,
        in_specs=[VMEM],
        out_specs=[VMEM] * 2,
        compiler_params=ROOM,
        cost_estimate=pl.CostEstimate(flops=COST, bytes_accessed=0, transcendentals=0),
        name="transform",
    )(parts)


def regroup(x, me, which):
    return jnp.concatenate(
        [x[pl.ds(pl.multiple_of(which(me, s) * MEMBERS, 8), MEMBERS), :] for s in range(GROUPS)], axis=0
    )


def coefficients(me, w_ref, turned):
    turned[...] = regroup(w_ref, me, group_from).T
    coeffs = regroup(turned, me, group_to).astype(jnp.bfloat16)
    return coeffs, 1.0 - jnp.sum(coeffs.astype(jnp.float32), axis=1, keepdims=True)


def mix(coeffs, keep, parts):
    stacked = jnp.concatenate([part.astype(jnp.float32) for part in parts], axis=0)
    center = jnp.sum(stacked, axis=0, keepdims=True) * (1.0 / K)
    mixed = jnp.dot(coeffs, stacked.astype(jnp.bfloat16), preferred_element_type=jnp.float32)
    return mixed + keep * center


def near_kernel(me_ref, w_ref, o0, o1, o2, o3, b0, b1, b2, b3, a0, a1, a2, a3, turned):
    coeffs, keep = coefficients(me_ref[0], w_ref, turned)
    for v in range(NEAR):
        parts = [ref[v] for ref in (o0, o1, o2, o3)] if v < VOBS else [ref[v - VOBS] for ref in (b0, b1, b2, b3)]
        mixed = mix(coeffs, keep, parts)
        for g, out in enumerate((a0, a1, a2, a3)):
            out[v] = mixed[g * MEMBERS : (g + 1) * MEMBERS].astype(jnp.bfloat16)


def analyse_near(me, weights, observed, bulk):
    return pl.pallas_call(
        near_kernel,
        out_shape=[jax.ShapeDtypeStruct((NEAR, MEMBERS, TILE), jnp.bfloat16)] * GROUPS,
        in_specs=[SMEM] + [VMEM] * 9,
        out_specs=[VMEM] * GROUPS,
        scratch_shapes=[pltpu.VMEM((K, K), jnp.float32)],
        compiler_params=ROOM,
        name="analyse_near",
    )(me, weights, *observed, *bulk)


def far_kernel(me_ref, w_ref, near_ref, b0, b1, b2, b3, out_ref, turned, result, sems):
    me = me_ref[0]
    cells = pl.ds(pl.multiple_of(me * TILE, TILE), TILE)
    copies = [pltpu.make_async_copy(near_ref, out_ref.at[pl.ds(0, NEAR), :, cells], sems.at[0])]
    copies[0].start()
    coeffs, keep = coefficients(me, w_ref, turned)
    for v in range(FAR):
        for c in range(GROUPS):
            parts = [ref[NEXT + c * FAR + v] for ref in (b0, b1, b2, b3)]
            mixed = mix(coeffs[:MEMBERS], keep[:MEMBERS], parts)
            result[v, :, pl.ds(c * TILE, TILE)] = mixed.astype(jnp.bfloat16)
        copies.append(pltpu.make_async_copy(result.at[v], out_ref.at[NEAR + v], sems.at[1 + v]))
        copies[-1].start()
    for copy in copies:
        copy.wait()


def analyse_far(me, weights, near, bulk):
    return pl.pallas_call(
        far_kernel,
        out_shape=jax.ShapeDtypeStruct((V, MEMBERS, GROUPS * TILE), jnp.bfloat16),
        in_specs=[SMEM] + [VMEM] * 6,
        out_specs=ANY,
        scratch_shapes=[
            pltpu.VMEM((K, K), jnp.float32),
            pltpu.VMEM((FAR, MEMBERS, GROUPS * TILE), jnp.bfloat16),
            pltpu.SemaphoreType.DMA((1 + FAR,)),
        ],
        compiler_params=ROOM,
        name="analyse_far",
    )(me, weights, near, *bulk)


def place_kernel(me_ref, c1, c2, c3, start_ref, out_ref, sems):
    del start_ref
    copies = []
    for s, chunk in enumerate((c1, c2, c3)):
        cells = pl.ds(pl.multiple_of(group_from(me_ref[0], s + 1) * TILE, TILE), TILE)
        copies.append(pltpu.make_async_copy(chunk, out_ref.at[pl.ds(0, NEAR), :, cells], sems.at[s]))
    for copy in copies:
        copy.start()
    for copy in copies:
        copy.wait()


def place(me, chunks, out):
    return pl.pallas_call(
        place_kernel,
        out_shape=jax.ShapeDtypeStruct(out.shape, out.dtype),
        in_specs=[SMEM] + [VMEM] * (GROUPS - 1) + [ANY],
        out_specs=ANY,
        scratch_shapes=[pltpu.SemaphoreType.DMA((GROUPS - 1,))],
        input_output_aliases={GROUPS: 0},
        compiler_params=ROOM,
        name="place",
    )(me, *chunks, out)


def ring(shift):
    return [(i, (i + shift) % GROUPS) for i in range(GROUPS)]


def scatter(chunks):
    return [chunks[0]] + [lax.ppermute(chunks[s], "member", ring(s)) for s in range(1, GROUPS)]


def exchange(copies, axes):
    return lax.all_to_all(copies, axes, 0, 0, tiled=True)


def total(folded):
    copies = exchange(spread_sum(folded[None], PLANE), ("x", "z"))
    copies = exchange(spread_sum(copies, COLUMN), ("member", "core"))
    return spread_sum(copies, 1)[0]


def body(prior, readings, error_spread, mapping, slots):
    member = lax.axis_index("member").astype(jnp.int32)
    me = member.reshape(1)
    prior = jnp.transpose(prior, (1, 0, 2))
    packed = pack(me, prior)
    observed = scatter(packed)
    bulk = scatter(pack_bulk(me, prior, packed[0]))
    folded = observe(me, slots.reshape(-1), observed, mapping[:, 0], readings[:, 0], error_spread[:, 0])
    folded = lax.fori_loop(0, jnp.where(member < GROUPS, 1, 2), lambda i, x: total(x), folded)
    weights, again = transform(folded)
    near = analyse_near(me, again, observed, bulk)
    arrived = scatter(near)
    out = analyse_far(me, again, near[0], bulk)
    out = place(me, arrived[1:], out)
    return (jnp.transpose(out, (1, 0, 2)), weights)


def solution(mesh):
    devices = mesh.devices.reshape(GROUPS, 4, 4, 2)
    axes = Mesh(devices, ("member", "x", "z", "core"))
    space = ("x", "z", "core")
    in_specs = (
        P("member", None, space),
        P(space, "member", None),
        P(space, "member", None),
        P(space, "member", None, None, None),
        P(space, "member", None),
    )
    out_specs = (P("member", None, space), P())
    return jax.shard_map(body, mesh=axes, in_specs=in_specs, out_specs=out_specs, check_vma=False)
```

```python
import functools

import jax
import jax.numpy as jnp
from jax import lax
from jax.experimental import pallas as pl
from jax.experimental.pallas import tpu as pltpu
from jax.sharding import Mesh
from jax.sharding import PartitionSpec as P

K = 96
V = 12
VOBS = 4
MEMBERS = 24
GROUPS = 4
TILE = 512
BLOCKS = 12
NNZ = 2
NS_ITERS = 4
HALF = K // 2
PLANE = 16
COLUMN = 8
NEAR = 6
COST = 40_000_000_000
FAR = V - NEAR
NEXT = NEAR - VOBS

EXACT = lax.Precision.HIGHEST
VMEM = pl.BlockSpec(memory_space=pltpu.VMEM)
SMEM = pl.BlockSpec(memory_space=pltpu.SMEM)
HBM = pl.BlockSpec(memory_space=pltpu.HBM)
ANY = pl.BlockSpec(memory_space=pl.ANY)
ROOM = pltpu.CompilerParams(vmem_limit_bytes=8 * 1024 * 1024)


def group_from(me, shift):
    return lax.rem(me + GROUPS - shift, GROUPS)


def group_to(me, shift):
    return lax.rem(me + shift, GROUPS)


def pack_kernel(me_ref, prior_ref, *refs):
    outs, sems = refs[:-1], refs[-1]
    copies = []
    for s in range(GROUPS):
        cells = pl.ds(pl.multiple_of(group_to(me_ref[0], s) * TILE, TILE), TILE)
        copies.append(pltpu.make_async_copy(prior_ref.at[pl.ds(0, VOBS), :, cells], outs[s], sems.at[s]))
    for copy in copies:
        copy.start()
    for copy in copies:
        copy.wait()


def pack(me, prior):
    return pl.pallas_call(
        pack_kernel,
        out_shape=[jax.ShapeDtypeStruct((VOBS, MEMBERS, TILE), prior.dtype)] * GROUPS,
        in_specs=[SMEM, HBM],
        out_specs=[VMEM] * GROUPS,
        scratch_shapes=[pltpu.SemaphoreType.DMA((GROUPS,))],
        compiler_params=ROOM,
        name="pack",
    )(me, prior)


def pack_bulk_kernel(me_ref, prior_ref, after_ref, *refs):
    del after_ref
    outs, sems = refs[:-1], refs[-1]
    copies = []
    for s, out in enumerate(outs, 1):
        cells = pl.ds(pl.multiple_of(group_to(me_ref[0], s) * TILE, TILE), TILE)
        copies.append((prior_ref.at[pl.ds(VOBS, NEXT), :, cells], out.at[pl.ds(0, NEXT)]))
        for c in range(GROUPS):
            source = prior_ref.at[pl.ds(NEAR, FAR), :, pl.ds(c * TILE, TILE)]
            copies.append((source, out.at[pl.ds(NEXT + c * FAR, FAR)]))
    copies = [pltpu.make_async_copy(*pair, sems.at[n]) for n, pair in enumerate(copies)]
    for copy in copies:
        copy.start()
    for copy in copies:
        copy.wait()


def pack_bulk(me, prior, after):
    return pl.pallas_call(
        pack_bulk_kernel,
        out_shape=[jax.ShapeDtypeStruct((NEXT + GROUPS * FAR, MEMBERS, TILE), prior.dtype)] * (GROUPS - 1),
        in_specs=[SMEM, ANY, ANY],
        out_specs=[HBM] * (GROUPS - 1),
        scratch_shapes=[pltpu.SemaphoreType.DMA(((GROUPS - 1) * (GROUPS + 1),))],
        compiler_params=ROOM,
        name="pack_bulk",
    )(me, prior, after)


def indices():
    row = lax.broadcasted_iota(jnp.int32, (HALF, 128), 0)
    lane = lax.broadcasted_iota(jnp.int32, (HALF, 128), 1)
    return row, lane


def fold(gram):
    row, lane = indices()
    top, low = gram[:HALF], gram[HALF:]
    second = pltpu.roll(low, 128 - HALF, 1)
    diagonal = jnp.sum(jnp.where(lane == row, second, 0.0), axis=1, keepdims=True)
    tail = jnp.sum(jnp.where(lane == HALF, second, 0.0), axis=1, keepdims=True)
    out = jnp.where((lane < HALF) & (lane > row), second, top)
    out = jnp.where(lane == K + 1, tail, out)
    return jnp.where(lane == K + 2, diagonal, out)


def unfold(folded):
    row, lane = indices()
    turned = jnp.concatenate([folded, jnp.zeros((128 - HALF, 128), jnp.float32)], axis=0).T
    flipped = turned[:HALF]
    first = jnp.where(lane <= row, folded, flipped)
    diagonal = folded[:, K + 2 : K + 3]
    second = jnp.where(lane < row, flipped, jnp.where(lane == row, diagonal, folded))
    top = jnp.where(lane < HALF, first, folded)
    low = jnp.where(lane < HALF, turned[HALF:K], pltpu.roll(second, HALF, 1))
    gram = jnp.concatenate([top, low], axis=0)[:, :K]
    projected = jnp.concatenate([folded[:, K : K + 1], folded[:, K + 1 : K + 2]], axis=0)
    return gram, projected


def observe_kernel(me_ref, slots_ref, c0, c1, c2, c3, op_ref, y_ref, var_ref, out_ref, state, spread, scaled):
    me = me_ref[0]
    for s, chunk in enumerate((c0, c1, c2, c3)):
        rows = pl.ds(pl.multiple_of(group_from(me, s) * MEMBERS, 8), MEMBERS)
        for v in range(VOBS):
            for c in range(TILE // 128):
                state[v * (TILE // 128) + c, rows, :] = chunk[v, :, c * 128 : (c + 1) * 128].astype(jnp.float32)
    spread[K:, :] = jnp.zeros((128 - K, BLOCKS * 128), jnp.float32)
    for b in range(BLOCKS):
        pred = jnp.zeros((K, 128), jnp.float32)
        for j in range(NNZ):
            part = state[slots_ref[b * NNZ + j]].astype(jnp.bfloat16)
            pred += lax.dot_general(
                part, op_ref[b, j], (((1,), (1,)), ((), ())), preferred_element_type=jnp.float32
            )
        mean = jnp.sum(pred, axis=0, keepdims=True) * (1.0 / K)
        dev = pred - mean
        lanes = pl.ds(b * 128, 128)
        spread[:K, lanes] = dev
        spread[K : K + 1, lanes] = y_ref[b : b + 1, :] - mean
        scaled[:, lanes] = dev / var_ref[b : b + 1, :]
    gram = lax.dot_general(
        scaled[...], spread[...], (((1,), (1,)), ((), ())), precision=EXACT, preferred_element_type=jnp.float32
    )
    out_ref[...] = fold(gram)


def observe(me, slots, chunks, op, values, variances):
    return pl.pallas_call(
        observe_kernel,
        out_shape=jax.ShapeDtypeStruct((HALF, 128), jnp.float32),
        in_specs=[SMEM, SMEM] + [VMEM] * 7,
        out_specs=VMEM,
        scratch_shapes=[
            pltpu.VMEM((VOBS * TILE // 128, K, 128), jnp.float32),
            pltpu.VMEM((128, BLOCKS * 128), jnp.float32),
            pltpu.VMEM((K, BLOCKS * 128), jnp.float32),
        ],
        compiler_params=ROOM,
        name="observe",
    )(me, slots, *chunks, op, values, variances)


def split(a):
    high = a.astype(jnp.bfloat16)
    return high, (a - high.astype(jnp.float32)).astype(jnp.bfloat16)


def fine_dot(a, b):
    a_high, a_low = split(a)
    b_high, b_low = split(b)
    small = jnp.dot(a_high, b_low, preferred_element_type=jnp.float32)
    small += jnp.dot(a_low, b_high, preferred_element_type=jnp.float32)
    return small + jnp.dot(a_high, b_high, preferred_element_type=jnp.float32)


def spread_kernel(parts_ref, out_ref):
    total = parts_ref[0]
    for part in range(1, parts_ref.shape[0]):
        total = total + parts_ref[part]
    for copy in range(out_ref.shape[0]):
        out_ref[copy] = total


def spread_sum(parts, copies):
    return pl.pallas_call(
        spread_kernel,
        out_shape=jax.ShapeDtypeStruct((copies, HALF, 128), jnp.float32),
        in_specs=[VMEM],
        out_specs=VMEM,
        compiler_params=ROOM,
        name="spread_sum",
    )(parts)


def transform_kernel(parts_ref, weights_ref, again_ref):
    folded = parts_ref[...]
    gram, projected = unfold(folded)
    row = lax.broadcasted_iota(jnp.int32, (K, K), 0)
    col = lax.broadcasted_iota(jnp.int32, (K, K), 1)
    eye = jnp.where(row == col, 1.0, 0.0).astype(jnp.float32)
    system = gram + (K - 1.0) * eye
    frob = jnp.sqrt(jnp.sum(system * system, keepdims=True))
    root = system / frob
    inverse = None
    for step in range(NS_ITERS):
        product = root if inverse is None else fine_dot(inverse, root)
        factor = 1.5 * eye - 0.5 * product
        if step < NS_ITERS - 1:
            root = fine_dot(root, factor)
        inverse = factor if inverse is None else fine_dot(factor, inverse)
    inverse_root = inverse / jnp.sqrt(frob)
    halfway = jnp.sum(inverse_root * projected, axis=0, keepdims=True)
    mean_shift = jnp.sum(inverse_root * halfway, axis=1, keepdims=True)
    weights = mean_shift + (K - 1.0) ** 0.5 * inverse_root
    weights_ref[...] = weights
    again_ref[...] = weights


def transform(parts):
    return pl.pallas_call(
        transform_kernel,
        out_shape=[jax.ShapeDtypeStruct((K, K), jnp.float32)] * 2,
        in_specs=[VMEM],
        out_specs=[VMEM] * 2,
        compiler_params=ROOM,
        cost_estimate=pl.CostEstimate(flops=COST, bytes_accessed=0, transcendentals=0),
        name="transform",
    )(parts)


def regroup(x, me, which):
    return jnp.concatenate(
        [x[pl.ds(pl.multiple_of(which(me, s) * MEMBERS, 8), MEMBERS), :] for s in range(GROUPS)], axis=0
    )


def coefficients(me, w_ref, turned):
    turned[...] = regroup(w_ref, me, group_from).T
    coeffs = regroup(turned, me, group_to).astype(jnp.bfloat16)
    return coeffs, 1.0 - jnp.sum(coeffs.astype(jnp.float32), axis=1, keepdims=True)


def mix(coeffs, keep, parts):
    stacked = jnp.concatenate([part.astype(jnp.float32) for part in parts], axis=0)
    center = jnp.sum(stacked, axis=0, keepdims=True) * (1.0 / K)
    mixed = jnp.dot(coeffs, stacked.astype(jnp.bfloat16), preferred_element_type=jnp.float32)
    return mixed + keep * center


def near_kernel(me_ref, w_ref, prior_ref, o1, o2, o3, b1, b2, b3, a0, a1, a2, a3, turned):
    coeffs, keep = coefficients(me_ref[0], w_ref, turned)
    cells = pl.ds(pl.multiple_of(me_ref[0] * TILE, TILE), TILE)
    for v in range(NEAR):
        parts = [ref[v] for ref in (o1, o2, o3)] if v < VOBS else [ref[v - VOBS] for ref in (b1, b2, b3)]
        parts = [prior_ref[v, :, cells]] + parts
        mixed = mix(coeffs, keep, parts)
        for g, out in enumerate((a0, a1, a2, a3)):
            out[v] = mixed[g * MEMBERS : (g + 1) * MEMBERS].astype(jnp.bfloat16)


def analyse_near(me, weights, prior, observed, bulk):
    return pl.pallas_call(
        near_kernel,
        out_shape=[jax.ShapeDtypeStruct((NEAR, MEMBERS, TILE), jnp.bfloat16)] * GROUPS,
        in_specs=[SMEM] + [VMEM] * 8,
        out_specs=[VMEM] * GROUPS,
        scratch_shapes=[pltpu.VMEM((K, K), jnp.float32)],
        compiler_params=ROOM,
        name="analyse_near",
    )(me, weights, prior, *observed, *bulk)


def far_kernel(me_ref, w_ref, near_ref, prior_ref, b1, b2, b3, out_ref, turned, result, sems):
    me = me_ref[0]
    cells = pl.ds(pl.multiple_of(me * TILE, TILE), TILE)
    copies = [pltpu.make_async_copy(near_ref, out_ref.at[pl.ds(0, NEAR), :, cells], sems.at[0])]
    copies[0].start()
    coeffs, keep = coefficients(me, w_ref, turned)
    for v in range(FAR):
        for c in range(GROUPS):
            lanes = pl.ds(c * TILE, TILE)
            parts = [prior_ref[NEAR + v, :, lanes]] + [ref[NEXT + c * FAR + v] for ref in (b1, b2, b3)]
            mixed = mix(coeffs[:MEMBERS], keep[:MEMBERS], parts)
            result[v, :, lanes] = mixed.astype(jnp.bfloat16)
        copies.append(pltpu.make_async_copy(result.at[v], out_ref.at[NEAR + v], sems.at[1 + v]))
        copies[-1].start()
    for copy in copies:
        copy.wait()


def analyse_far(me, weights, near, prior, bulk):
    return pl.pallas_call(
        far_kernel,
        out_shape=jax.ShapeDtypeStruct((V, MEMBERS, GROUPS * TILE), jnp.bfloat16),
        in_specs=[SMEM] + [VMEM] * 6,
        out_specs=ANY,
        scratch_shapes=[
            pltpu.VMEM((K, K), jnp.float32),
            pltpu.VMEM((FAR, MEMBERS, GROUPS * TILE), jnp.bfloat16),
            pltpu.SemaphoreType.DMA((1 + FAR,)),
        ],
        compiler_params=ROOM,
        name="analyse_far",
    )(me, weights, near, prior, *bulk)


def place_kernel(me_ref, c1, c2, c3, start_ref, out_ref, sems):
    del start_ref
    copies = []
    for s, chunk in enumerate((c1, c2, c3)):
        cells = pl.ds(pl.multiple_of(group_from(me_ref[0], s + 1) * TILE, TILE), TILE)
        copies.append(pltpu.make_async_copy(chunk, out_ref.at[pl.ds(0, NEAR), :, cells], sems.at[s]))
    for copy in copies:
        copy.start()
    for copy in copies:
        copy.wait()


def place(me, chunks, out):
    return pl.pallas_call(
        place_kernel,
        out_shape=jax.ShapeDtypeStruct(out.shape, out.dtype),
        in_specs=[SMEM] + [VMEM] * (GROUPS - 1) + [ANY],
        out_specs=ANY,
        scratch_shapes=[pltpu.SemaphoreType.DMA((GROUPS - 1,))],
        input_output_aliases={GROUPS: 0},
        compiler_params=ROOM,
        name="place",
    )(me, *chunks, out)


def ring(shift):
    return [(i, (i + shift) % GROUPS) for i in range(GROUPS)]


def scatter(chunks):
    return [lax.ppermute(chunk, "member", ring(s)) for s, chunk in enumerate(chunks, 1)]


def exchange(copies, axes):
    return lax.all_to_all(copies, axes, 0, 0, tiled=True)


def total(folded):
    copies = exchange(spread_sum(folded[None], PLANE), ("x", "z"))
    copies = exchange(spread_sum(copies, COLUMN), ("member", "core"))
    return spread_sum(copies, 1)[0]


def body(prior, readings, error_spread, mapping, slots):
    member = lax.axis_index("member").astype(jnp.int32)
    me = member.reshape(1)
    prior = jnp.transpose(prior, (1, 0, 2))
    packed = pack(me, prior)
    observed = scatter(packed[1:])
    bulk = scatter(pack_bulk(me, prior, packed[0]))
    folded = observe(
        me, slots.reshape(-1), [packed[0]] + observed, mapping[:, 0], readings[:, 0], error_spread[:, 0]
    )
    folded = lax.cond(member < GROUPS, total, lambda x: x, folded)
    weights, again = transform(folded)
    near = analyse_near(me, again, prior, observed, bulk)
    arrived = scatter(near[1:])
    out = place(me, arrived, analyse_far(me, again, near[0], prior, bulk))
    return (jnp.transpose(out, (1, 0, 2)), weights)


def solution(mesh):
    devices = mesh.devices.reshape(GROUPS, 4, 4, 2)
    axes = Mesh(devices, ("member", "x", "z", "core"))
    space = ("x", "z", "core")
    in_specs = (
        P("member", None, space),
        P(space, "member", None),
        P(space, "member", None),
        P(space, "member", None, None, None),
        P(space, "member", None),
    )
    out_specs = (P("member", None, space), P())
    return jax.shard_map(body, mesh=axes, in_specs=in_specs, out_specs=out_specs, check_vma=False)
```

```python
import functools

import jax
import jax.numpy as jnp
from jax import lax
from jax.experimental import pallas as pl
from jax.experimental.pallas import tpu as pltpu
from jax.sharding import Mesh
from jax.sharding import PartitionSpec as P

K = 96
V = 12
VOBS = 4
MEMBERS = 24
GROUPS = 4
TILE = 512
BLOCKS = 12
NNZ = 2
NS_ITERS = 4
HALF = K // 2
PLANE = 16
COLUMN = 8
NEAR = 6
COST = 40_000_000_000
FAR = V - NEAR
NEXT = NEAR - VOBS

EXACT = lax.Precision.HIGHEST
VMEM = pl.BlockSpec(memory_space=pltpu.VMEM)
SMEM = pl.BlockSpec(memory_space=pltpu.SMEM)
HBM = pl.BlockSpec(memory_space=pltpu.HBM)
ANY = pl.BlockSpec(memory_space=pl.ANY)
ROOM = pltpu.CompilerParams(vmem_limit_bytes=8 * 1024 * 1024)


def group_from(me, shift):
    return lax.rem(me + GROUPS - shift, GROUPS)


def group_to(me, shift):
    return lax.rem(me + shift, GROUPS)


def pack_kernel(me_ref, prior_ref, *refs):
    outs, sems = refs[:-1], refs[-1]
    copies = []
    for s in range(GROUPS):
        cells = pl.ds(pl.multiple_of(group_to(me_ref[0], s) * TILE, TILE), TILE)
        copies.append(pltpu.make_async_copy(prior_ref.at[pl.ds(0, VOBS), :, cells], outs[s], sems.at[s]))
    for copy in copies:
        copy.start()
    for copy in copies:
        copy.wait()


def pack(me, prior):
    return pl.pallas_call(
        pack_kernel,
        out_shape=[jax.ShapeDtypeStruct((VOBS, MEMBERS, TILE), prior.dtype)] * GROUPS,
        in_specs=[SMEM, HBM],
        out_specs=[VMEM] * GROUPS,
        scratch_shapes=[pltpu.SemaphoreType.DMA((GROUPS,))],
        compiler_params=ROOM,
        name="pack",
    )(me, prior)


def pack_bulk_kernel(me_ref, prior_ref, after_ref, *refs):
    del after_ref
    outs, sems = refs[:-1], refs[-1]
    copies = []
    for s, out in enumerate(outs, 1):
        cells = pl.ds(pl.multiple_of(group_to(me_ref[0], s) * TILE, TILE), TILE)
        copies.append((prior_ref.at[pl.ds(VOBS, NEXT), :, cells], out.at[pl.ds(0, NEXT)]))
        for c in range(GROUPS):
            source = prior_ref.at[pl.ds(NEAR, FAR), :, pl.ds(c * TILE, TILE)]
            copies.append((source, out.at[pl.ds(NEXT + c * FAR, FAR)]))
    copies = [pltpu.make_async_copy(*pair, sems.at[n]) for n, pair in enumerate(copies)]
    for copy in copies:
        copy.start()
    for copy in copies:
        copy.wait()


def pack_bulk(me, prior, after):
    return pl.pallas_call(
        pack_bulk_kernel,
        out_shape=[jax.ShapeDtypeStruct((NEXT + GROUPS * FAR, MEMBERS, TILE), prior.dtype)] * (GROUPS - 1),
        in_specs=[SMEM, ANY, ANY],
        out_specs=[HBM] * (GROUPS - 1),
        scratch_shapes=[pltpu.SemaphoreType.DMA(((GROUPS - 1) * (GROUPS + 1),))],
        compiler_params=ROOM,
        name="pack_bulk",
    )(me, prior, after)


def indices():
    row = lax.broadcasted_iota(jnp.int32, (HALF, 128), 0)
    lane = lax.broadcasted_iota(jnp.int32, (HALF, 128), 1)
    return row, lane


def fold(gram):
    row, lane = indices()
    top, low = gram[:HALF], gram[HALF:]
    second = pltpu.roll(low, 128 - HALF, 1)
    diagonal = jnp.sum(jnp.where(lane == row, second, 0.0), axis=1, keepdims=True)
    tail = jnp.sum(jnp.where(lane == HALF, second, 0.0), axis=1, keepdims=True)
    out = jnp.where((lane < HALF) & (lane > row), second, top)
    out = jnp.where(lane == K + 1, tail, out)
    return jnp.where(lane == K + 2, diagonal, out)


def unfold(folded):
    row, lane = indices()
    turned = jnp.concatenate([folded, jnp.zeros((128 - HALF, 128), jnp.float32)], axis=0).T
    flipped = turned[:HALF]
    first = jnp.where(lane <= row, folded, flipped)
    diagonal = folded[:, K + 2 : K + 3]
    second = jnp.where(lane < row, flipped, jnp.where(lane == row, diagonal, folded))
    top = jnp.where(lane < HALF, first, folded)
    low = jnp.where(lane < HALF, turned[HALF:K], pltpu.roll(second, HALF, 1))
    gram = jnp.concatenate([top, low], axis=0)[:, :K]
    projected = jnp.concatenate([folded[:, K : K + 1], folded[:, K + 1 : K + 2]], axis=0)
    return gram, projected


def split(a):
    high = a.astype(jnp.bfloat16)
    return high, (a - high.astype(jnp.float32)).astype(jnp.bfloat16)


def dot_rows(a, b):
    return lax.dot_general(a, b, (((1,), (1,)), ((), ())), preferred_element_type=jnp.float32)


def observe_kernel(me_ref, slots_ref, c0, c1, c2, c3, op_ref, y_ref, var_ref, out_ref, state):
    me = me_ref[0]
    for s, chunk in enumerate((c0, c1, c2, c3)):
        rows = pl.ds(pl.multiple_of(group_from(me, s) * MEMBERS, 8), MEMBERS)
        for v in range(VOBS):
            for c in range(TILE // 128):
                state[v * (TILE // 128) + c, rows, :] = chunk[v, :, c * 128 : (c + 1) * 128].astype(jnp.float32)
    spread, scaled = [], []
    projected = jnp.zeros((K, 128), jnp.float32)
    for b in range(BLOCKS):
        picked = [state[slots_ref[b * NNZ + j]].astype(jnp.bfloat16) for j in range(NNZ)]
        mapping = jnp.concatenate([op_ref[b, j] for j in range(NNZ)], axis=1)
        pred = dot_rows(jnp.concatenate(picked, axis=1), mapping)
        mean = jnp.sum(pred, axis=0, keepdims=True) * (1.0 / K)
        spread.append(pred - mean)
        scaled.append(spread[-1] * (1.0 / var_ref[b : b + 1, :]))
        projected += scaled[-1] * (y_ref[b : b + 1, :] - mean)
    high, low = split(jnp.concatenate(scaled, axis=1))
    spread_high, spread_low = split(jnp.concatenate(spread, axis=1))
    both = dot_rows(jnp.concatenate([high, low], axis=0), spread_high)
    gram = both[:K] + both[K:] + dot_rows(high, spread_low)
    projected = jnp.sum(projected, axis=1, keepdims=True)
    out_ref[...] = fold(jnp.concatenate([gram, projected, jnp.zeros((K, 127 - K), jnp.float32)], axis=1))


def observe(me, slots, chunks, op, values, variances):
    return pl.pallas_call(
        observe_kernel,
        out_shape=jax.ShapeDtypeStruct((HALF, 128), jnp.float32),
        in_specs=[SMEM, SMEM] + [VMEM] * 7,
        out_specs=VMEM,
        scratch_shapes=[pltpu.VMEM((VOBS * TILE // 128, K, 128), jnp.float32)],
        compiler_params=ROOM,
        name="observe",
    )(me, slots, *chunks, op, values, variances)


def fine_dot(a, b):
    a_high, a_low = split(a)
    b_high, b_low = split(b)
    small = jnp.dot(a_high, b_low, preferred_element_type=jnp.float32)
    small += jnp.dot(a_low, b_high, preferred_element_type=jnp.float32)
    return small + jnp.dot(a_high, b_high, preferred_element_type=jnp.float32)


def spread_kernel(parts_ref, out_ref):
    total = parts_ref[0]
    for part in range(1, parts_ref.shape[0]):
        total = total + parts_ref[part]
    for copy in range(out_ref.shape[0]):
        out_ref[copy] = total


def spread_sum(parts, copies):
    return pl.pallas_call(
        spread_kernel,
        out_shape=jax.ShapeDtypeStruct((copies, HALF, 128), jnp.float32),
        in_specs=[VMEM],
        out_specs=VMEM,
        compiler_params=ROOM,
        name="spread_sum",
    )(parts)


def transform_kernel(parts_ref, weights_ref):
    folded = parts_ref[...]
    gram, projected = unfold(folded)
    row = lax.broadcasted_iota(jnp.int32, (K, K), 0)
    col = lax.broadcasted_iota(jnp.int32, (K, K), 1)
    eye = jnp.where(row == col, 1.0, 0.0).astype(jnp.float32)
    system = gram + (K - 1.0) * eye
    frob = jnp.sqrt(jnp.sum(system * system, keepdims=True))
    root = system / frob
    inverse = None
    for step in range(NS_ITERS):
        product = root if inverse is None else fine_dot(inverse, root)
        factor = 1.5 * eye - 0.5 * product
        if step < NS_ITERS - 1:
            root = fine_dot(root, factor)
        inverse = factor if inverse is None else fine_dot(factor, inverse)
    inverse_root = inverse / jnp.sqrt(frob)
    halfway = jnp.sum(inverse_root * projected, axis=0, keepdims=True)
    mean_shift = jnp.sum(inverse_root * halfway, axis=1, keepdims=True)
    weights_ref[...] = mean_shift + (K - 1.0) ** 0.5 * inverse_root


def transform(parts):
    return pl.pallas_call(
        transform_kernel,
        out_shape=jax.ShapeDtypeStruct((K, K), jnp.float32),
        in_specs=[VMEM],
        out_specs=VMEM,
        compiler_params=ROOM,
        cost_estimate=pl.CostEstimate(flops=COST, bytes_accessed=0, transcendentals=0),
        name="transform",
    )(parts)


def regroup(x, me, which):
    return jnp.concatenate(
        [x[pl.ds(pl.multiple_of(which(me, s) * MEMBERS, 8), MEMBERS), :] for s in range(GROUPS)], axis=0
    )


def coefficients(me, w_ref, turned):
    turned[...] = regroup(w_ref, me, group_from).T
    coeffs = regroup(turned, me, group_to).astype(jnp.bfloat16)
    return coeffs, 1.0 - jnp.sum(coeffs.astype(jnp.float32), axis=1, keepdims=True)


def mix(coeffs, keep, parts):
    stacked = jnp.concatenate([part.astype(jnp.float32) for part in parts], axis=0)
    center = jnp.sum(stacked, axis=0, keepdims=True) * (1.0 / K)
    mixed = jnp.dot(coeffs, stacked.astype(jnp.bfloat16), preferred_element_type=jnp.float32)
    return mixed + keep * center


def near_kernel(me_ref, w_ref, prior_ref, o1, o2, o3, b1, b2, b3, a0, a1, a2, a3, turned):
    coeffs, keep = coefficients(me_ref[0], w_ref, turned)
    cells = pl.ds(pl.multiple_of(me_ref[0] * TILE, TILE), TILE)
    for v in range(NEAR):
        parts = [ref[v] for ref in (o1, o2, o3)] if v < VOBS else [ref[v - VOBS] for ref in (b1, b2, b3)]
        parts = [prior_ref[v, :, cells]] + parts
        mixed = mix(coeffs, keep, parts)
        for g, out in enumerate((a0, a1, a2, a3)):
            out[v] = mixed[g * MEMBERS : (g + 1) * MEMBERS].astype(jnp.bfloat16)


def analyse_near(me, weights, prior, observed, bulk):
    return pl.pallas_call(
        near_kernel,
        out_shape=[jax.ShapeDtypeStruct((NEAR, MEMBERS, TILE), jnp.bfloat16)] * GROUPS,
        in_specs=[SMEM] + [VMEM] * 8,
        out_specs=[VMEM] * GROUPS,
        scratch_shapes=[pltpu.VMEM((K, K), jnp.float32)],
        compiler_params=ROOM,
        name="analyse_near",
    )(me, weights, prior, *observed, *bulk)


def far_kernel(me_ref, w_ref, near_ref, prior_ref, b1, b2, b3, out_ref, weights_ref, turned, result, sems):
    me = me_ref[0]
    cells = pl.ds(pl.multiple_of(me * TILE, TILE), TILE)
    copies = [
        pltpu.make_async_copy(near_ref, out_ref.at[pl.ds(0, NEAR), :, cells], sems.at[0]),
        pltpu.make_async_copy(w_ref, weights_ref, sems.at[1]),
    ]
    for copy in copies:
        copy.start()
    coeffs, keep = coefficients(me, w_ref, turned)
    for v in range(FAR):
        for c in range(GROUPS):
            lanes = pl.ds(c * TILE, TILE)
            parts = [prior_ref[NEAR + v, :, lanes]] + [ref[NEXT + c * FAR + v] for ref in (b1, b2, b3)]
            mixed = mix(coeffs[:MEMBERS], keep[:MEMBERS], parts)
            result[v, :, lanes] = mixed.astype(jnp.bfloat16)
        copies.append(pltpu.make_async_copy(result.at[v], out_ref.at[NEAR + v], sems.at[2 + v]))
        copies[-1].start()
    for copy in copies:
        copy.wait()


def analyse_far(me, weights, near, prior, bulk):
    return pl.pallas_call(
        far_kernel,
        out_shape=[
            jax.ShapeDtypeStruct((V, MEMBERS, GROUPS * TILE), jnp.bfloat16),
            jax.ShapeDtypeStruct((K, K), jnp.float32),
        ],
        in_specs=[SMEM] + [VMEM] * 6,
        out_specs=[ANY, ANY],
        scratch_shapes=[
            pltpu.VMEM((K, K), jnp.float32),
            pltpu.VMEM((FAR, MEMBERS, GROUPS * TILE), jnp.bfloat16),
            pltpu.SemaphoreType.DMA((2 + FAR,)),
        ],
        compiler_params=ROOM,
        name="analyse_far",
    )(me, weights, near, prior, *bulk)


def place_kernel(me_ref, c1, c2, c3, start_ref, out_ref, sems):
    del start_ref
    copies = []
    for s, chunk in enumerate((c1, c2, c3)):
        cells = pl.ds(pl.multiple_of(group_from(me_ref[0], s + 1) * TILE, TILE), TILE)
        copies.append(pltpu.make_async_copy(chunk, out_ref.at[pl.ds(0, NEAR), :, cells], sems.at[s]))
    for copy in copies:
        copy.start()
    for copy in copies:
        copy.wait()


def place(me, chunks, out):
    return pl.pallas_call(
        place_kernel,
        out_shape=jax.ShapeDtypeStruct(out.shape, out.dtype),
        in_specs=[SMEM] + [VMEM] * (GROUPS - 1) + [ANY],
        out_specs=ANY,
        scratch_shapes=[pltpu.SemaphoreType.DMA((GROUPS - 1,))],
        input_output_aliases={GROUPS: 0},
        compiler_params=ROOM,
        name="place",
    )(me, *chunks, out)


def ring(shift):
    return [(i, (i + shift) % GROUPS) for i in range(GROUPS)]


def scatter(chunks):
    return [lax.ppermute(chunk, "member", ring(s)) for s, chunk in enumerate(chunks, 1)]


def exchange(copies, axes):
    return lax.all_to_all(copies, axes, 0, 0, tiled=True)


def total(folded):
    copies = exchange(spread_sum(folded[None], PLANE), ("x", "z"))
    copies = exchange(spread_sum(copies, COLUMN), ("member", "core"))
    return spread_sum(copies, 1)[0]


def body(prior, readings, error_spread, mapping, slots):
    member = lax.axis_index("member").astype(jnp.int32)
    me = member.reshape(1)
    prior = jnp.transpose(prior, (1, 0, 2))
    packed = pack(me, prior)
    observed = scatter(packed[1:])
    bulk = scatter(pack_bulk(me, prior, packed[0]))
    folded = observe(
        me, slots.reshape(-1), [packed[0]] + observed, mapping[:, 0], readings[:, 0], error_spread[:, 0]
    )
    folded = lax.cond(member < GROUPS, total, lambda x: x, folded)
    weights = transform(folded)
    near = analyse_near(me, weights, prior, observed, bulk)
    arrived = scatter(near[1:])
    out, weights = analyse_far(me, weights, near[0], prior, bulk)
    return (jnp.transpose(place(me, arrived, out), (1, 0, 2)), weights)


def solution(mesh):
    devices = mesh.devices.reshape(GROUPS, 4, 4, 2)
    axes = Mesh(devices, ("member", "x", "z", "core"))
    space = ("x", "z", "core")
    in_specs = (
        P("member", None, space),
        P(space, "member", None),
        P(space, "member", None),
        P(space, "member", None, None, None),
        P(space, "member", None),
    )
    out_specs = (P("member", None, space), P())
    return jax.shard_map(body, mesh=axes, in_specs=in_specs, out_specs=out_specs, check_vma=False)
```

```python
import functools

import jax
import jax.numpy as jnp
from jax import lax
from jax.experimental import pallas as pl
from jax.experimental.pallas import tpu as pltpu
from jax.sharding import Mesh
from jax.sharding import PartitionSpec as P

K = 96
V = 12
VOBS = 4
MEMBERS = 24
GROUPS = 4
TILE = 512
BLOCKS = 12
NNZ = 2
NS_ITERS = 4
HALF = K // 2
PLANE = 16
COLUMN = 8
NEAR = 8
COST = 40_000_000_000
FAR = V - NEAR
NEXT = NEAR - VOBS

EXACT = lax.Precision.HIGHEST
VMEM = pl.BlockSpec(memory_space=pltpu.VMEM)
SMEM = pl.BlockSpec(memory_space=pltpu.SMEM)
HBM = pl.BlockSpec(memory_space=pltpu.HBM)
ANY = pl.BlockSpec(memory_space=pl.ANY)
ROOM = pltpu.CompilerParams(vmem_limit_bytes=8 * 1024 * 1024)


def group_from(me, shift):
    return lax.rem(me + GROUPS - shift, GROUPS)


def group_to(me, shift):
    return lax.rem(me + shift, GROUPS)


def pack_kernel(me_ref, prior_ref, *refs):
    outs, sems = refs[:-1], refs[-1]
    copies = []
    for s in range(GROUPS):
        cells = pl.ds(pl.multiple_of(group_to(me_ref[0], s) * TILE, TILE), TILE)
        copies.append(pltpu.make_async_copy(prior_ref.at[pl.ds(0, VOBS), :, cells], outs[s], sems.at[s]))
    for copy in copies:
        copy.start()
    for copy in copies:
        copy.wait()


def pack(me, prior):
    return pl.pallas_call(
        pack_kernel,
        out_shape=[jax.ShapeDtypeStruct((VOBS, MEMBERS, TILE), prior.dtype)] * GROUPS,
        in_specs=[SMEM, HBM],
        out_specs=[VMEM] * GROUPS,
        scratch_shapes=[pltpu.SemaphoreType.DMA((GROUPS,))],
        compiler_params=ROOM,
        name="pack",
    )(me, prior)


def pack_bulk_kernel(me_ref, prior_ref, after_ref, *refs):
    del after_ref
    outs, sems = refs[:-1], refs[-1]
    copies = []
    for s, out in enumerate(outs, 1):
        cells = pl.ds(pl.multiple_of(group_to(me_ref[0], s) * TILE, TILE), TILE)
        copies.append((prior_ref.at[pl.ds(VOBS, NEXT), :, cells], out.at[pl.ds(0, NEXT)]))
        for c in range(GROUPS):
            source = prior_ref.at[pl.ds(NEAR, FAR), :, pl.ds(c * TILE, TILE)]
            copies.append((source, out.at[pl.ds(NEXT + c * FAR, FAR)]))
    copies = [pltpu.make_async_copy(*pair, sems.at[n]) for n, pair in enumerate(copies)]
    for copy in copies:
        copy.start()
    for copy in copies:
        copy.wait()


def pack_bulk(me, prior, after):
    return pl.pallas_call(
        pack_bulk_kernel,
        out_shape=[jax.ShapeDtypeStruct((NEXT + GROUPS * FAR, MEMBERS, TILE), prior.dtype)] * (GROUPS - 1),
        in_specs=[SMEM, ANY, ANY],
        out_specs=[HBM] * (GROUPS - 1),
        scratch_shapes=[pltpu.SemaphoreType.DMA(((GROUPS - 1) * (GROUPS + 1),))],
        compiler_params=ROOM,
        name="pack_bulk",
    )(me, prior, after)


def indices():
    row = lax.broadcasted_iota(jnp.int32, (HALF, 128), 0)
    lane = lax.broadcasted_iota(jnp.int32, (HALF, 128), 1)
    return row, lane


def fold(gram):
    row, lane = indices()
    top, low = gram[:HALF], gram[HALF:]
    second = pltpu.roll(low, 128 - HALF, 1)
    diagonal = jnp.sum(jnp.where(lane == row, second, 0.0), axis=1, keepdims=True)
    tail = jnp.sum(jnp.where(lane == HALF, second, 0.0), axis=1, keepdims=True)
    out = jnp.where((lane < HALF) & (lane > row), second, top)
    out = jnp.where(lane == K + 1, tail, out)
    return jnp.where(lane == K + 2, diagonal, out)


def unfold(folded):
    row, lane = indices()
    turned = jnp.concatenate([folded, jnp.zeros((128 - HALF, 128), jnp.float32)], axis=0).T
    flipped = turned[:HALF]
    first = jnp.where(lane <= row, folded, flipped)
    diagonal = folded[:, K + 2 : K + 3]
    second = jnp.where(lane < row, flipped, jnp.where(lane == row, diagonal, folded))
    top = jnp.where(lane < HALF, first, folded)
    low = jnp.where(lane < HALF, turned[HALF:K], pltpu.roll(second, HALF, 1))
    gram = jnp.concatenate([top, low], axis=0)[:, :K]
    projected = jnp.concatenate([folded[:, K : K + 1], folded[:, K + 1 : K + 2]], axis=0)
    return gram, projected


def split(a):
    high = a.astype(jnp.bfloat16)
    return high, (a - high.astype(jnp.float32)).astype(jnp.bfloat16)


def dot_rows(a, b):
    return lax.dot_general(a, b, (((1,), (1,)), ((), ())), preferred_element_type=jnp.float32)


def observe_kernel(me_ref, slots_ref, c0, c1, c2, c3, op_ref, y_ref, var_ref, out_ref, state):
    me = me_ref[0]
    for s, chunk in enumerate((c0, c1, c2, c3)):
        rows = pl.ds(pl.multiple_of(group_from(me, s) * MEMBERS, 8), MEMBERS)
        for v in range(VOBS):
            for c in range(TILE // 128):
                state[v * (TILE // 128) + c, rows, :] = chunk[v, :, c * 128 : (c + 1) * 128].astype(jnp.float32)
    spread, scaled = [], []
    projected = jnp.zeros((K, 128), jnp.float32)
    for b in range(BLOCKS):
        picked = [state[slots_ref[b * NNZ + j]].astype(jnp.bfloat16) for j in range(NNZ)]
        mapping = jnp.concatenate([op_ref[b, j] for j in range(NNZ)], axis=1)
        pred = dot_rows(jnp.concatenate(picked, axis=1), mapping)
        mean = jnp.sum(pred, axis=0, keepdims=True) * (1.0 / K)
        spread.append(pred - mean)
        scaled.append(spread[-1] * (1.0 / var_ref[b : b + 1, :]))
        projected += scaled[-1] * (y_ref[b : b + 1, :] - mean)
    high, low = split(jnp.concatenate(scaled, axis=1))
    spread_high, spread_low = split(jnp.concatenate(spread, axis=1))
    both = dot_rows(jnp.concatenate([high, low], axis=0), spread_high)
    gram = both[:K] + both[K:] + dot_rows(high, spread_low)
    projected = jnp.sum(projected, axis=1, keepdims=True)
    out_ref[...] = fold(jnp.concatenate([gram, projected, jnp.zeros((K, 127 - K), jnp.float32)], axis=1))


def observe(me, slots, chunks, op, values, variances):
    return pl.pallas_call(
        observe_kernel,
        out_shape=jax.ShapeDtypeStruct((HALF, 128), jnp.float32),
        in_specs=[SMEM, SMEM] + [VMEM] * 7,
        out_specs=VMEM,
        scratch_shapes=[pltpu.VMEM((VOBS * TILE // 128, K, 128), jnp.float32)],
        compiler_params=ROOM,
        name="observe",
    )(me, slots, *chunks, op, values, variances)


def fine_dot(a, b):
    a_high, a_low = split(a)
    b_high, b_low = split(b)
    small = jnp.dot(a_high, b_low, preferred_element_type=jnp.float32)
    small += jnp.dot(a_low, b_high, preferred_element_type=jnp.float32)
    return small + jnp.dot(a_high, b_high, preferred_element_type=jnp.float32)


def narrow(folded):
    _, lane = indices()
    high = folded.astype(jnp.bfloat16).astype(jnp.float32)
    low = pltpu.roll(folded - high, 3, 1)
    return jnp.where((lane >= K + 3) & (lane < K + 6), low, high).astype(jnp.bfloat16)


def widen(total):
    _, lane = indices()
    return jnp.where((lane >= K) & (lane < K + 3), total + pltpu.roll(total, 125, 1), total)


def spread_kernel(parts_ref, out_ref):
    total = parts_ref[0].astype(jnp.float32)
    for part in range(1, parts_ref.shape[0]):
        total = total + parts_ref[part].astype(jnp.float32)
    if parts_ref.dtype == jnp.bfloat16:
        total = widen(total)
    if out_ref.dtype == jnp.bfloat16:
        total = narrow(total)
    for copy in range(out_ref.shape[0]):
        out_ref[copy] = total


def spread_sum(parts, copies, dtype=jnp.float32):
    return pl.pallas_call(
        spread_kernel,
        out_shape=jax.ShapeDtypeStruct((copies, HALF, 128), dtype),
        in_specs=[VMEM],
        out_specs=VMEM,
        compiler_params=ROOM,
        name="spread_sum",
    )(parts)


def transform_kernel(parts_ref, weights_ref):
    folded = parts_ref[...]
    gram, projected = unfold(folded)
    row = lax.broadcasted_iota(jnp.int32, (K, K), 0)
    col = lax.broadcasted_iota(jnp.int32, (K, K), 1)
    eye = jnp.where(row == col, 1.0, 0.0).astype(jnp.float32)
    system = gram + (K - 1.0) * eye
    frob = jnp.sqrt(jnp.sum(system * system, keepdims=True))
    root = system / frob
    inverse = None
    for step in range(NS_ITERS):
        product = root if inverse is None else fine_dot(inverse, root)
        factor = 1.5 * eye - 0.5 * product
        if step < NS_ITERS - 1:
            root = fine_dot(root, factor)
        inverse = factor if inverse is None else fine_dot(factor, inverse)
    inverse_root = inverse / jnp.sqrt(frob)
    halfway = jnp.sum(inverse_root * projected, axis=0, keepdims=True)
    mean_shift = jnp.sum(inverse_root * halfway, axis=1, keepdims=True)
    weights_ref[...] = mean_shift + (K - 1.0) ** 0.5 * inverse_root


def transform(parts):
    return pl.pallas_call(
        transform_kernel,
        out_shape=jax.ShapeDtypeStruct((K, K), jnp.float32),
        in_specs=[VMEM],
        out_specs=VMEM,
        compiler_params=ROOM,
        cost_estimate=pl.CostEstimate(flops=COST, bytes_accessed=0, transcendentals=0),
        name="transform",
    )(parts)


def regroup(x, me, which):
    return jnp.concatenate(
        [x[pl.ds(pl.multiple_of(which(me, s) * MEMBERS, 8), MEMBERS), :] for s in range(GROUPS)], axis=0
    )


def coefficients(me, w_ref, turned):
    turned[...] = regroup(w_ref, me, group_from).T
    coeffs = regroup(turned, me, group_to).astype(jnp.bfloat16)
    return coeffs, 1.0 - jnp.sum(coeffs.astype(jnp.float32), axis=1, keepdims=True)


def mix(coeffs, keep, parts):
    stacked = jnp.concatenate([part.astype(jnp.float32) for part in parts], axis=0)
    center = jnp.sum(stacked, axis=0, keepdims=True) * (1.0 / K)
    mixed = jnp.dot(coeffs, stacked.astype(jnp.bfloat16), preferred_element_type=jnp.float32)
    return mixed + keep * center


def near_kernel(me_ref, w_ref, prior_ref, o1, o2, o3, b1, b2, b3, a0, a1, a2, a3, turned):
    coeffs, keep = coefficients(me_ref[0], w_ref, turned)
    cells = pl.ds(pl.multiple_of(me_ref[0] * TILE, TILE), TILE)
    for v in range(NEAR):
        parts = [ref[v] for ref in (o1, o2, o3)] if v < VOBS else [ref[v - VOBS] for ref in (b1, b2, b3)]
        parts = [prior_ref[v, :, cells]] + parts
        mixed = mix(coeffs, keep, parts)
        for g, out in enumerate((a0, a1, a2, a3)):
            out[v] = mixed[g * MEMBERS : (g + 1) * MEMBERS].astype(jnp.bfloat16)


def analyse_near(me, weights, prior, observed, bulk):
    return pl.pallas_call(
        near_kernel,
        out_shape=[jax.ShapeDtypeStruct((NEAR, MEMBERS, TILE), jnp.bfloat16)] * GROUPS,
        in_specs=[SMEM] + [VMEM] * 8,
        out_specs=[VMEM] * GROUPS,
        scratch_shapes=[pltpu.VMEM((K, K), jnp.float32)],
        compiler_params=ROOM,
        name="analyse_near",
    )(me, weights, prior, *observed, *bulk)


def far_kernel(me_ref, w_ref, near_ref, prior_ref, b1, b2, b3, out_ref, weights_ref, turned, result, sems):
    me = me_ref[0]
    cells = pl.ds(pl.multiple_of(me * TILE, TILE), TILE)
    copies = [
        pltpu.make_async_copy(near_ref, out_ref.at[pl.ds(0, NEAR), :, cells], sems.at[0]),
        pltpu.make_async_copy(w_ref, weights_ref, sems.at[1]),
    ]
    for copy in copies:
        copy.start()
    coeffs, keep = coefficients(me, w_ref, turned)
    for v in range(FAR):
        for c in range(GROUPS):
            lanes = pl.ds(c * TILE, TILE)
            parts = [prior_ref[NEAR + v, :, lanes]] + [ref[NEXT + c * FAR + v] for ref in (b1, b2, b3)]
            mixed = mix(coeffs[:MEMBERS], keep[:MEMBERS], parts)
            result[v, :, lanes] = mixed.astype(jnp.bfloat16)
        copies.append(pltpu.make_async_copy(result.at[v], out_ref.at[NEAR + v], sems.at[2 + v]))
        copies[-1].start()
    for copy in copies:
        copy.wait()


def analyse_far(me, weights, near, prior, bulk):
    return pl.pallas_call(
        far_kernel,
        out_shape=[
            jax.ShapeDtypeStruct((V, MEMBERS, GROUPS * TILE), jnp.bfloat16),
            jax.ShapeDtypeStruct((K, K), jnp.float32),
        ],
        in_specs=[SMEM] + [VMEM] * 6,
        out_specs=[ANY, ANY],
        scratch_shapes=[
            pltpu.VMEM((K, K), jnp.float32),
            pltpu.VMEM((FAR, MEMBERS, GROUPS * TILE), jnp.bfloat16),
            pltpu.SemaphoreType.DMA((2 + FAR,)),
        ],
        compiler_params=ROOM,
        name="analyse_far",
    )(me, weights, near, prior, *bulk)


def place_kernel(me_ref, c1, c2, c3, start_ref, out_ref, sems):
    del start_ref
    copies = []
    for s, chunk in enumerate((c1, c2, c3)):
        cells = pl.ds(pl.multiple_of(group_from(me_ref[0], s + 1) * TILE, TILE), TILE)
        copies.append(pltpu.make_async_copy(chunk, out_ref.at[pl.ds(0, NEAR), :, cells], sems.at[s]))
    for copy in copies:
        copy.start()
    for copy in copies:
        copy.wait()


def place(me, chunks, out):
    return pl.pallas_call(
        place_kernel,
        out_shape=jax.ShapeDtypeStruct(out.shape, out.dtype),
        in_specs=[SMEM] + [VMEM] * (GROUPS - 1) + [ANY],
        out_specs=ANY,
        scratch_shapes=[pltpu.SemaphoreType.DMA((GROUPS - 1,))],
        input_output_aliases={GROUPS: 0},
        compiler_params=ROOM,
        name="place",
    )(me, *chunks, out)


def ring(shift):
    return [(i, (i + shift) % GROUPS) for i in range(GROUPS)]


def scatter(chunks):
    return [lax.ppermute(chunk, "member", ring(s)) for s, chunk in enumerate(chunks, 1)]


def exchange(copies, axes):
    return lax.all_to_all(copies, axes, 0, 0, tiled=True)


def total(folded):
    copies = exchange(spread_sum(folded[None], PLANE, jnp.bfloat16), ("x", "z"))
    copies = exchange(spread_sum(copies, COLUMN), ("member", "core"))
    return spread_sum(copies, 1)[0]


def body(prior, readings, error_spread, mapping, slots):
    member = lax.axis_index("member").astype(jnp.int32)
    me = member.reshape(1)
    prior = jnp.transpose(prior, (1, 0, 2))
    packed = pack(me, prior)
    observed = scatter(packed[1:])
    bulk = scatter(pack_bulk(me, prior, packed[0]))
    folded = observe(
        me, slots.reshape(-1), [packed[0]] + observed, mapping[:, 0], readings[:, 0], error_spread[:, 0]
    )
    folded = lax.cond(member < GROUPS, total, lambda x: x, folded)
    weights = transform(folded)
    near = analyse_near(me, weights, prior, observed, bulk)
    arrived = scatter(near[1:])
    out, weights = analyse_far(me, weights, near[0], prior, bulk)
    return (jnp.transpose(place(me, arrived, out), (1, 0, 2)), weights)


def solution(mesh):
    devices = mesh.devices.reshape(GROUPS, 4, 4, 2)
    axes = Mesh(devices, ("member", "x", "z", "core"))
    space = ("x", "z", "core")
    in_specs = (
        P("member", None, space),
        P(space, "member", None),
        P(space, "member", None),
        P(space, "member", None, None, None),
        P(space, "member", None),
    )
    out_specs = (P("member", None, space), P())
    return jax.shard_map(body, mesh=axes, in_specs=in_specs, out_specs=out_specs, check_vma=False)
```

```python
import functools

import jax
import jax.numpy as jnp
from jax import lax
from jax.experimental import pallas as pl
from jax.experimental.pallas import tpu as pltpu
from jax.sharding import Mesh
from jax.sharding import PartitionSpec as P

K = 96
V = 12
VOBS = 4
MEMBERS = 24
GROUPS = 4
TILE = 512
BLOCKS = 12
NNZ = 2
NS_ITERS = 4
HALF = K // 2
PLANE = 16
COLUMN = 8
NEAR = 7
COST = 40_000_000_000
FAR = V - NEAR
NEXT = NEAR - VOBS

EXACT = lax.Precision.HIGHEST
VMEM = pl.BlockSpec(memory_space=pltpu.VMEM)
SMEM = pl.BlockSpec(memory_space=pltpu.SMEM)
HBM = pl.BlockSpec(memory_space=pltpu.HBM)
ANY = pl.BlockSpec(memory_space=pl.ANY)
ROOM = pltpu.CompilerParams(vmem_limit_bytes=8 * 1024 * 1024)


def group_from(me, shift):
    return lax.rem(me + GROUPS - shift, GROUPS)


def group_to(me, shift):
    return lax.rem(me + shift, GROUPS)


def pack_kernel(me_ref, prior_ref, *refs):
    outs, sems = refs[:-1], refs[-1]
    copies = []
    for s in range(GROUPS):
        cells = pl.ds(pl.multiple_of(group_to(me_ref[0], s) * TILE, TILE), TILE)
        copies.append(pltpu.make_async_copy(prior_ref.at[pl.ds(0, VOBS), :, cells], outs[s], sems.at[s]))
    for copy in copies:
        copy.start()
    for copy in copies:
        copy.wait()


def pack(me, prior):
    return pl.pallas_call(
        pack_kernel,
        out_shape=[jax.ShapeDtypeStruct((VOBS, MEMBERS, TILE), prior.dtype)] * GROUPS,
        in_specs=[SMEM, HBM],
        out_specs=[VMEM] * GROUPS,
        scratch_shapes=[pltpu.SemaphoreType.DMA((GROUPS,))],
        compiler_params=ROOM,
        name="pack",
    )(me, prior)


def pack_bulk_kernel(me_ref, prior_ref, after_ref, *refs):
    del after_ref
    outs, sems = refs[:-1], refs[-1]
    copies = []
    for s, out in enumerate(outs, 1):
        cells = pl.ds(pl.multiple_of(group_to(me_ref[0], s) * TILE, TILE), TILE)
        copies.append((prior_ref.at[pl.ds(VOBS, NEXT), :, cells], out.at[pl.ds(0, NEXT)]))
        for c in range(GROUPS):
            source = prior_ref.at[pl.ds(NEAR, FAR), :, pl.ds(c * TILE, TILE)]
            copies.append((source, out.at[pl.ds(NEXT + c * FAR, FAR)]))
    copies = [pltpu.make_async_copy(*pair, sems.at[n]) for n, pair in enumerate(copies)]
    for copy in copies:
        copy.start()
    for copy in copies:
        copy.wait()


def pack_bulk(me, prior, after):
    return pl.pallas_call(
        pack_bulk_kernel,
        out_shape=[jax.ShapeDtypeStruct((NEXT + GROUPS * FAR, MEMBERS, TILE), prior.dtype)] * (GROUPS - 1),
        in_specs=[SMEM, ANY, ANY],
        out_specs=[HBM] * (GROUPS - 1),
        scratch_shapes=[pltpu.SemaphoreType.DMA(((GROUPS - 1) * (GROUPS + 1),))],
        compiler_params=ROOM,
        name="pack_bulk",
    )(me, prior, after)


def indices():
    row = lax.broadcasted_iota(jnp.int32, (HALF, 128), 0)
    lane = lax.broadcasted_iota(jnp.int32, (HALF, 128), 1)
    return row, lane


def fold(gram):
    row, lane = indices()
    top, low = gram[:HALF], gram[HALF:]
    second = pltpu.roll(low, 128 - HALF, 1)
    diagonal = jnp.sum(jnp.where(lane == row, second, 0.0), axis=1, keepdims=True)
    tail = jnp.sum(jnp.where(lane == HALF, second, 0.0), axis=1, keepdims=True)
    out = jnp.where((lane < HALF) & (lane > row), second, top)
    out = jnp.where(lane == K + 1, tail, out)
    return jnp.where(lane == K + 2, diagonal, out)


def unfold(folded):
    row, lane = indices()
    turned = jnp.concatenate([folded, jnp.zeros((128 - HALF, 128), jnp.float32)], axis=0).T
    flipped = turned[:HALF]
    first = jnp.where(lane <= row, folded, flipped)
    diagonal = folded[:, K + 2 : K + 3]
    second = jnp.where(lane < row, flipped, jnp.where(lane == row, diagonal, folded))
    top = jnp.where(lane < HALF, first, folded)
    low = jnp.where(lane < HALF, turned[HALF:K], pltpu.roll(second, HALF, 1))
    gram = jnp.concatenate([top, low], axis=0)[:, :K]
    projected = jnp.concatenate([folded[:, K : K + 1], folded[:, K + 1 : K + 2]], axis=0)
    return gram, projected


def split(a):
    high = a.astype(jnp.bfloat16)
    return high, (a - high.astype(jnp.float32)).astype(jnp.bfloat16)


def dot_rows(a, b):
    return lax.dot_general(a, b, (((1,), (1,)), ((), ())), preferred_element_type=jnp.float32)


def observe_kernel(me_ref, slots_ref, c0, c1, c2, c3, op_ref, y_ref, var_ref, out_ref, state):
    me = me_ref[0]
    for s, chunk in enumerate((c0, c1, c2, c3)):
        rows = pl.ds(pl.multiple_of(group_from(me, s) * MEMBERS, 8), MEMBERS)
        for v in range(VOBS):
            for c in range(TILE // 128):
                state[v * (TILE // 128) + c, rows, :] = chunk[v, :, c * 128 : (c + 1) * 128].astype(jnp.float32)
    spread, scaled = [], []
    projected = jnp.zeros((K, 128), jnp.float32)
    for b in range(BLOCKS):
        picked = [state[slots_ref[j, b]].astype(jnp.bfloat16) for j in range(NNZ)]
        mapping = jnp.concatenate([op_ref[b, j] for j in range(NNZ)], axis=1)
        pred = dot_rows(jnp.concatenate(picked, axis=1), mapping)
        mean = jnp.sum(pred, axis=0, keepdims=True) * (1.0 / K)
        spread.append(pred - mean)
        scaled.append(spread[-1] * (1.0 / var_ref[b]))
        projected += scaled[-1] * (y_ref[b] - mean)
    high, low = split(jnp.concatenate(scaled, axis=1))
    spread_high, spread_low = split(jnp.concatenate(spread, axis=1))
    both = dot_rows(jnp.concatenate([high, low], axis=0), spread_high)
    gram = both[:K] + both[K:] + dot_rows(high, spread_low)
    projected = jnp.sum(projected, axis=1, keepdims=True)
    out_ref[...] = fold(jnp.concatenate([gram, projected, jnp.zeros((K, 127 - K), jnp.float32)], axis=1))


def observe(me, slots, chunks, op, values, variances):
    return pl.pallas_call(
        observe_kernel,
        out_shape=jax.ShapeDtypeStruct((HALF, 128), jnp.float32),
        in_specs=[SMEM, SMEM] + [VMEM] * 7,
        out_specs=VMEM,
        scratch_shapes=[pltpu.VMEM((VOBS * TILE // 128, K, 128), jnp.float32)],
        compiler_params=ROOM,
        name="observe",
    )(me, slots, *chunks, op, values, variances)


def fine_dot(a, b):
    a_high, a_low = split(a)
    b_high, b_low = split(b)
    small = jnp.dot(a_high, b_low, preferred_element_type=jnp.float32)
    small += jnp.dot(a_low, b_high, preferred_element_type=jnp.float32)
    return small + jnp.dot(a_high, b_high, preferred_element_type=jnp.float32)


def narrow(folded):
    _, lane = indices()
    high = folded.astype(jnp.bfloat16).astype(jnp.float32)
    low = pltpu.roll(folded - high, 3, 1)
    return jnp.where((lane >= K + 3) & (lane < K + 6), low, high).astype(jnp.bfloat16)


def widen(total):
    _, lane = indices()
    return jnp.where((lane >= K) & (lane < K + 3), total + pltpu.roll(total, 125, 1), total)


def spread_kernel(parts_ref, out_ref):
    total = parts_ref[0].astype(jnp.float32)
    for part in range(1, parts_ref.shape[0]):
        total = total + parts_ref[part].astype(jnp.float32)
    if parts_ref.dtype == jnp.bfloat16:
        total = widen(total)
    if out_ref.dtype == jnp.bfloat16:
        total = narrow(total)
    for copy in range(out_ref.shape[0]):
        out_ref[copy] = total


def spread_sum(parts, copies, dtype=jnp.float32):
    return pl.pallas_call(
        spread_kernel,
        out_shape=jax.ShapeDtypeStruct((copies, HALF, 128), dtype),
        in_specs=[VMEM],
        out_specs=VMEM,
        compiler_params=ROOM,
        name="spread_sum",
    )(parts)


def transform_kernel(parts_ref, weights_ref):
    folded = parts_ref[...]
    gram, projected = unfold(folded)
    row = lax.broadcasted_iota(jnp.int32, (K, K), 0)
    col = lax.broadcasted_iota(jnp.int32, (K, K), 1)
    eye = jnp.where(row == col, 1.0, 0.0).astype(jnp.float32)
    system = gram + (K - 1.0) * eye
    frob = jnp.sqrt(jnp.sum(system * system, keepdims=True))
    root = system / frob
    inverse = None
    for step in range(NS_ITERS):
        product = root if inverse is None else fine_dot(inverse, root)
        factor = 1.5 * eye - 0.5 * product
        if step < NS_ITERS - 1:
            root = fine_dot(root, factor)
        inverse = factor if inverse is None else fine_dot(factor, inverse)
    inverse_root = inverse / jnp.sqrt(frob)
    halfway = jnp.sum(inverse_root * projected, axis=0, keepdims=True)
    mean_shift = jnp.sum(inverse_root * halfway, axis=1, keepdims=True)
    weights_ref[...] = mean_shift + (K - 1.0) ** 0.5 * inverse_root


def transform(parts):
    return pl.pallas_call(
        transform_kernel,
        out_shape=jax.ShapeDtypeStruct((K, K), jnp.float32),
        in_specs=[VMEM],
        out_specs=VMEM,
        compiler_params=ROOM,
        cost_estimate=pl.CostEstimate(flops=COST, bytes_accessed=0, transcendentals=0),
        name="transform",
    )(parts)


def regroup(x, me, which):
    return jnp.concatenate(
        [x[pl.ds(pl.multiple_of(which(me, s) * MEMBERS, 8), MEMBERS), :] for s in range(GROUPS)], axis=0
    )


def coefficients(me, w_ref, turned):
    turned[...] = regroup(w_ref, me, group_from).T
    coeffs = regroup(turned, me, group_to).astype(jnp.bfloat16)
    return coeffs, 1.0 - jnp.sum(coeffs.astype(jnp.float32), axis=1, keepdims=True)


def mix(coeffs, keep, parts):
    stacked = jnp.concatenate([part.astype(jnp.float32) for part in parts], axis=0)
    center = jnp.sum(stacked, axis=0, keepdims=True) * (1.0 / K)
    mixed = jnp.dot(coeffs, stacked.astype(jnp.bfloat16), preferred_element_type=jnp.float32)
    return mixed + keep * center


def near_kernel(me_ref, w_ref, prior_ref, o1, o2, o3, b1, b2, b3, a0, a1, a2, a3, turned):
    coeffs, keep = coefficients(me_ref[0], w_ref, turned)
    cells = pl.ds(pl.multiple_of(me_ref[0] * TILE, TILE), TILE)
    for v in range(NEAR):
        parts = [ref[v] for ref in (o1, o2, o3)] if v < VOBS else [ref[v - VOBS] for ref in (b1, b2, b3)]
        parts = [prior_ref[v, :, cells]] + parts
        mixed = mix(coeffs, keep, parts)
        for g, out in enumerate((a0, a1, a2, a3)):
            out[v] = mixed[g * MEMBERS : (g + 1) * MEMBERS].astype(jnp.bfloat16)


def analyse_near(me, weights, prior, observed, bulk):
    return pl.pallas_call(
        near_kernel,
        out_shape=[jax.ShapeDtypeStruct((NEAR, MEMBERS, TILE), jnp.bfloat16)] * GROUPS,
        in_specs=[SMEM] + [VMEM] * 8,
        out_specs=[VMEM] * GROUPS,
        scratch_shapes=[pltpu.VMEM((K, K), jnp.float32)],
        compiler_params=ROOM,
        name="analyse_near",
    )(me, weights, prior, *observed, *bulk)


def far_kernel(me_ref, w_ref, near_ref, prior_ref, b1, b2, b3, out_ref, weights_ref, turned, result, sems):
    me = me_ref[0]
    cells = pl.ds(pl.multiple_of(me * TILE, TILE), TILE)
    copies = [
        pltpu.make_async_copy(near_ref, out_ref.at[pl.ds(0, NEAR), :, cells], sems.at[0]),
        pltpu.make_async_copy(w_ref, weights_ref, sems.at[1]),
    ]
    for copy in copies:
        copy.start()
    coeffs, keep = coefficients(me, w_ref, turned)
    for v in range(FAR):
        for c in range(GROUPS):
            lanes = pl.ds(c * TILE, TILE)
            parts = [prior_ref[NEAR + v, :, lanes]] + [ref[NEXT + c * FAR + v] for ref in (b1, b2, b3)]
            mixed = mix(coeffs[:MEMBERS], keep[:MEMBERS], parts)
            result[v, :, lanes] = mixed.astype(jnp.bfloat16)
        copies.append(pltpu.make_async_copy(result.at[v], out_ref.at[NEAR + v], sems.at[2 + v]))
        copies[-1].start()
    for copy in copies:
        copy.wait()


def analyse_far(me, weights, near, prior, bulk):
    return pl.pallas_call(
        far_kernel,
        out_shape=[
            jax.ShapeDtypeStruct((V, MEMBERS, GROUPS * TILE), jnp.bfloat16),
            jax.ShapeDtypeStruct((K, K), jnp.float32),
        ],
        in_specs=[SMEM] + [VMEM] * 6,
        out_specs=[ANY, ANY],
        scratch_shapes=[
            pltpu.VMEM((K, K), jnp.float32),
            pltpu.VMEM((FAR, MEMBERS, GROUPS * TILE), jnp.bfloat16),
            pltpu.SemaphoreType.DMA((2 + FAR,)),
        ],
        compiler_params=ROOM,
        name="analyse_far",
    )(me, weights, near, prior, *bulk)


def place_kernel(me_ref, c1, c2, c3, start_ref, out_ref, sems):
    del start_ref
    copies = []
    for s, chunk in enumerate((c1, c2, c3)):
        cells = pl.ds(pl.multiple_of(group_from(me_ref[0], s + 1) * TILE, TILE), TILE)
        copies.append(pltpu.make_async_copy(chunk, out_ref.at[pl.ds(0, NEAR), :, cells], sems.at[s]))
    for copy in copies:
        copy.start()
    for copy in copies:
        copy.wait()


def place(me, chunks, out):
    return pl.pallas_call(
        place_kernel,
        out_shape=jax.ShapeDtypeStruct(out.shape, out.dtype),
        in_specs=[SMEM] + [VMEM] * (GROUPS - 1) + [ANY],
        out_specs=ANY,
        scratch_shapes=[pltpu.SemaphoreType.DMA((GROUPS - 1,))],
        input_output_aliases={GROUPS: 0},
        compiler_params=ROOM,
        name="place",
    )(me, *chunks, out)


def ring(shift):
    return [(i, (i + shift) % GROUPS) for i in range(GROUPS)]


def scatter(chunks):
    return [lax.ppermute(chunk, "member", ring(s)) for s, chunk in enumerate(chunks, 1)]


def exchange(copies, axes):
    return lax.all_to_all(copies, axes, 0, 0, tiled=True)


def total(folded):
    copies = exchange(spread_sum(folded[None], PLANE, jnp.bfloat16), ("x", "z"))
    copies = exchange(spread_sum(copies, COLUMN), ("member", "core"))
    return spread_sum(copies, 1)[0]


def body(prior, readings, error_spread, mapping, slots):
    member = lax.axis_index("member").astype(jnp.int32)
    me = member.reshape(1)
    prior = jnp.transpose(prior, (1, 0, 2))
    packed = pack(me, prior)
    observed = scatter(packed[1:])
    bulk = scatter(pack_bulk(me, prior, packed[0]))
    folded = observe(
        me, jnp.transpose(slots, (1, 2, 0))[0], [packed[0]] + observed, mapping[:, 0], readings, error_spread
    )
    folded = lax.cond(member < GROUPS, total, lambda x: x, folded)
    weights = transform(folded)
    near = analyse_near(me, weights, prior, observed, bulk)
    arrived = scatter(near[1:])
    out, weights = analyse_far(me, weights, near[0], prior, bulk)
    return (jnp.transpose(place(me, arrived, out), (1, 0, 2)), weights)


def solution(mesh):
    devices = mesh.devices.reshape(GROUPS, 4, 4, 2)
    axes = Mesh(devices, ("member", "x", "z", "core"))
    space = ("x", "z", "core")
    in_specs = (
        P("member", None, space),
        P(space, "member", None),
        P(space, "member", None),
        P(space, "member", None, None, None),
        P(space, "member", None),
    )
    out_specs = (P("member", None, space), P())
    return jax.shard_map(body, mesh=axes, in_specs=in_specs, out_specs=out_specs, check_vma=False)
```

```python
import functools

import jax
import jax.numpy as jnp
from jax import lax
from jax.experimental import pallas as pl
from jax.experimental.pallas import tpu as pltpu
from jax.sharding import Mesh
from jax.sharding import PartitionSpec as P

K = 96
V = 12
VOBS = 4
MEMBERS = 24
GROUPS = 4
TILE = 512
BLOCKS = 12
NNZ = 2
NS_ITERS = 4
HALF = K // 2
PLANE = 16
COLUMN = 8
NEAR = 7
COST = 40_000_000_000
FAR = V - NEAR
NEXT = NEAR - VOBS

EXACT = lax.Precision.HIGHEST
VMEM = pl.BlockSpec(memory_space=pltpu.VMEM)
SMEM = pl.BlockSpec(memory_space=pltpu.SMEM)
HBM = pl.BlockSpec(memory_space=pltpu.HBM)
ANY = pl.BlockSpec(memory_space=pl.ANY)
ROOM = pltpu.CompilerParams(vmem_limit_bytes=8 * 1024 * 1024)


def group_from(me, shift):
    return lax.rem(me + GROUPS - shift, GROUPS)


def group_to(me, shift):
    return lax.rem(me + shift, GROUPS)


def pack_kernel(me_ref, prior_ref, *refs):
    outs, sems = refs[:-1], refs[-1]
    copies = []
    for s in range(GROUPS):
        cells = pl.ds(pl.multiple_of(group_to(me_ref[0], s) * TILE, TILE), TILE)
        copies.append(pltpu.make_async_copy(prior_ref.at[pl.ds(0, VOBS), :, cells], outs[s], sems.at[s]))
    for copy in copies:
        copy.start()
    for copy in copies:
        copy.wait()


def pack(me, prior):
    return pl.pallas_call(
        pack_kernel,
        out_shape=[jax.ShapeDtypeStruct((VOBS, MEMBERS, TILE), prior.dtype)] * GROUPS,
        in_specs=[SMEM, HBM],
        out_specs=[VMEM] * GROUPS,
        scratch_shapes=[pltpu.SemaphoreType.DMA((GROUPS,))],
        compiler_params=ROOM,
        name="pack",
    )(me, prior)


def pack_bulk_kernel(me_ref, prior_ref, after_ref, *refs):
    del after_ref
    outs, sems = refs[:-1], refs[-1]
    copies = []
    for s, out in enumerate(outs, 1):
        cells = pl.ds(pl.multiple_of(group_to(me_ref[0], s) * TILE, TILE), TILE)
        copies.append((prior_ref.at[pl.ds(VOBS, NEXT), :, cells], out.at[pl.ds(0, NEXT)]))
        for c in range(GROUPS):
            source = prior_ref.at[pl.ds(NEAR, FAR), :, pl.ds(c * TILE, TILE)]
            copies.append((source, out.at[pl.ds(NEXT + c * FAR, FAR)]))
    copies = [pltpu.make_async_copy(*pair, sems.at[n]) for n, pair in enumerate(copies)]
    for copy in copies:
        copy.start()
    for copy in copies:
        copy.wait()


def pack_bulk(me, prior, after):
    return pl.pallas_call(
        pack_bulk_kernel,
        out_shape=[jax.ShapeDtypeStruct((NEXT + GROUPS * FAR, MEMBERS, TILE), prior.dtype)] * (GROUPS - 1),
        in_specs=[SMEM, ANY, ANY],
        out_specs=[HBM] * (GROUPS - 1),
        scratch_shapes=[pltpu.SemaphoreType.DMA(((GROUPS - 1) * (GROUPS + 1),))],
        compiler_params=ROOM,
        name="pack_bulk",
    )(me, prior, after)


def indices():
    row = lax.broadcasted_iota(jnp.int32, (HALF, 128), 0)
    lane = lax.broadcasted_iota(jnp.int32, (HALF, 128), 1)
    return row, lane


def fold(gram):
    row, lane = indices()
    top, low = gram[:HALF], gram[HALF:]
    second = pltpu.roll(low, 128 - HALF, 1)
    diagonal = jnp.sum(jnp.where(lane == row, second, 0.0), axis=1, keepdims=True)
    tail = jnp.sum(jnp.where(lane == HALF, second, 0.0), axis=1, keepdims=True)
    out = jnp.where((lane < HALF) & (lane > row), second, top)
    out = jnp.where(lane == K + 1, tail, out)
    return jnp.where(lane == K + 2, diagonal, out)


def unfold(folded):
    row, lane = indices()
    turned = jnp.concatenate([folded, jnp.zeros((128 - HALF, 128), jnp.float32)], axis=0).T
    flipped = turned[:HALF]
    first = jnp.where(lane <= row, folded, flipped)
    diagonal = folded[:, K + 2 : K + 3]
    second = jnp.where(lane < row, flipped, jnp.where(lane == row, diagonal, folded))
    top = jnp.where(lane < HALF, first, folded)
    low = jnp.where(lane < HALF, turned[HALF:K], pltpu.roll(second, HALF, 1))
    gram = jnp.concatenate([top, low], axis=0)[:, :K]
    projected = jnp.concatenate([folded[:, K : K + 1], folded[:, K + 1 : K + 2]], axis=0)
    return gram, projected


def split(a):
    high = a.astype(jnp.bfloat16)
    return high, (a - high.astype(jnp.float32)).astype(jnp.bfloat16)


def dot_rows(a, b):
    return lax.dot_general(a, b, (((1,), (1,)), ((), ())), preferred_element_type=jnp.float32)


def observe_kernel(me_ref, slots_ref, c0, c1, c2, c3, op_ref, y_ref, var_ref, out_ref, state):
    me = me_ref[0]
    for s, chunk in enumerate((c0, c1, c2, c3)):
        rows = pl.ds(pl.multiple_of(group_from(me, s) * MEMBERS, 8), MEMBERS)
        for v in range(VOBS):
            for c in range(TILE // 128):
                state[v * (TILE // 128) + c, rows, :] = chunk[v, :, c * 128 : (c + 1) * 128].astype(jnp.float32)
    spread, scaled = [], []
    projected = jnp.zeros((K, 128), jnp.float32)
    for b in range(BLOCKS):
        picked = [state[slots_ref[j, b]].astype(jnp.bfloat16) for j in range(NNZ)]
        mapping = jnp.concatenate([op_ref[b, j] for j in range(NNZ)], axis=1)
        pred = dot_rows(jnp.concatenate(picked, axis=1), mapping)
        mean = jnp.sum(pred, axis=0, keepdims=True) * (1.0 / K)
        spread.append(pred - mean)
        scaled.append(spread[-1] * (1.0 / var_ref[b]))
        projected += scaled[-1] * (y_ref[b] - mean)
    high, low = split(jnp.concatenate(scaled, axis=1))
    spread_high, spread_low = split(jnp.concatenate(spread, axis=1))
    both = dot_rows(jnp.concatenate([high, low], axis=0), spread_high)
    gram = both[:K] + both[K:] + dot_rows(high, spread_low)
    projected = jnp.sum(projected, axis=1, keepdims=True)
    out_ref[...] = fold(jnp.concatenate([gram, projected, jnp.zeros((K, 127 - K), jnp.float32)], axis=1))


def observe(me, slots, chunks, op, values, variances):
    return pl.pallas_call(
        observe_kernel,
        out_shape=jax.ShapeDtypeStruct((HALF, 128), jnp.float32),
        in_specs=[SMEM, SMEM] + [VMEM] * 7,
        out_specs=VMEM,
        scratch_shapes=[pltpu.VMEM((VOBS * TILE // 128, K, 128), jnp.float32)],
        compiler_params=ROOM,
        name="observe",
    )(me, slots, *chunks, op, values, variances)


def fine_dot(a, b):
    a_high, a_low = split(a)
    b_high, b_low = split(b)
    small = jnp.dot(a_high, b_low, preferred_element_type=jnp.float32)
    small += jnp.dot(a_low, b_high, preferred_element_type=jnp.float32)
    return small + jnp.dot(a_high, b_high, preferred_element_type=jnp.float32)


def narrow(folded):
    _, lane = indices()
    high = folded.astype(jnp.bfloat16).astype(jnp.float32)
    low = pltpu.roll(folded - high, 3, 1)
    return jnp.where((lane >= K + 3) & (lane < K + 6), low, high).astype(jnp.bfloat16)


def widen(total):
    _, lane = indices()
    return jnp.where((lane >= K) & (lane < K + 3), total + pltpu.roll(total, 125, 1), total)


def spread_kernel(parts_ref, out_ref):
    total = parts_ref[0].astype(jnp.float32)
    for part in range(1, parts_ref.shape[0]):
        total = total + parts_ref[part].astype(jnp.float32)
    if parts_ref.dtype == jnp.bfloat16:
        total = widen(total)
    if out_ref.dtype == jnp.bfloat16:
        total = narrow(total)
    for copy in range(out_ref.shape[0]):
        out_ref[copy] = total


def spread_sum(parts, copies, dtype=jnp.float32):
    return pl.pallas_call(
        spread_kernel,
        out_shape=jax.ShapeDtypeStruct((copies, HALF, 128), dtype),
        in_specs=[VMEM],
        out_specs=VMEM,
        compiler_params=ROOM,
        name="spread_sum",
    )(parts)


def transform_kernel(parts_ref, weights_ref):
    folded = parts_ref[...]
    gram, projected = unfold(folded)
    row = lax.broadcasted_iota(jnp.int32, (K, K), 0)
    col = lax.broadcasted_iota(jnp.int32, (K, K), 1)
    eye = jnp.where(row == col, 1.0, 0.0).astype(jnp.float32)
    system = gram + (K - 1.0) * eye
    frob = jnp.sqrt(jnp.sum(system * system, keepdims=True))
    root = system / frob
    inverse = None
    for step in range(NS_ITERS):
        product = root if inverse is None else fine_dot(inverse, root)
        factor = 1.5 * eye - 0.5 * product
        if step < NS_ITERS - 1:
            root = fine_dot(root, factor)
        inverse = factor if inverse is None else fine_dot(factor, inverse)
    inverse_root = inverse / jnp.sqrt(frob)
    halfway = jnp.sum(inverse_root * projected, axis=0, keepdims=True)
    mean_shift = jnp.sum(inverse_root * halfway, axis=1, keepdims=True)
    weights_ref[...] = mean_shift + (K - 1.0) ** 0.5 * inverse_root


def transform(parts):
    return pl.pallas_call(
        transform_kernel,
        out_shape=jax.ShapeDtypeStruct((K, K), jnp.float32),
        in_specs=[VMEM],
        out_specs=VMEM,
        compiler_params=ROOM,
        cost_estimate=pl.CostEstimate(flops=COST, bytes_accessed=0, transcendentals=0),
        name="transform",
    )(parts)


def regroup(x, me, which):
    return jnp.concatenate(
        [x[pl.ds(pl.multiple_of(which(me, s) * MEMBERS, 8), MEMBERS), :] for s in range(GROUPS)], axis=0
    )


def coefficients(me, w_ref, turned):
    turned[...] = regroup(w_ref, me, group_from).T
    coeffs = regroup(turned, me, group_to).astype(jnp.bfloat16)
    return coeffs, 1.0 - jnp.sum(coeffs.astype(jnp.float32), axis=1, keepdims=True)


def mix(coeffs, keep, parts):
    stacked = jnp.concatenate([part.astype(jnp.float32) for part in parts], axis=0)
    center = jnp.sum(stacked, axis=0, keepdims=True) * (1.0 / K)
    mixed = jnp.dot(coeffs, stacked.astype(jnp.bfloat16), preferred_element_type=jnp.float32)
    return mixed + keep * center


def near_kernel(me_ref, w_ref, prior_ref, o1, o2, o3, b1, b2, b3, a0, a1, a2, a3, turned):
    coeffs, keep = coefficients(me_ref[0], w_ref, turned)
    cells = pl.ds(pl.multiple_of(me_ref[0] * TILE, TILE), TILE)
    for v in range(NEAR):
        parts = [ref[v] for ref in (o1, o2, o3)] if v < VOBS else [ref[v - VOBS] for ref in (b1, b2, b3)]
        parts = [prior_ref[v, :, cells]] + parts
        mixed = mix(coeffs, keep, parts)
        for g, out in enumerate((a0, a1, a2, a3)):
            out[v] = mixed[g * MEMBERS : (g + 1) * MEMBERS].astype(jnp.bfloat16)


def analyse_near(me, weights, prior, observed, bulk):
    return pl.pallas_call(
        near_kernel,
        out_shape=[jax.ShapeDtypeStruct((NEAR, MEMBERS, TILE), jnp.bfloat16)] * GROUPS,
        in_specs=[SMEM] + [VMEM] * 8,
        out_specs=[VMEM] * GROUPS,
        scratch_shapes=[pltpu.VMEM((K, K), jnp.float32)],
        compiler_params=ROOM,
        name="analyse_near",
    )(me, weights, prior, *observed, *bulk)


def far_kernel(me_ref, w_ref, near_ref, prior_ref, b1, b2, b3, out_ref, weights_ref, turned, result, sems):
    me = me_ref[0]
    cells = pl.ds(pl.multiple_of(me * TILE, TILE), TILE)
    copies = [
        pltpu.make_async_copy(near_ref, out_ref.at[pl.ds(0, NEAR), :, cells], sems.at[0]),
        pltpu.make_async_copy(w_ref, weights_ref, sems.at[1]),
    ]
    for copy in copies:
        copy.start()
    coeffs, keep = coefficients(me, w_ref, turned)
    for v in range(FAR):
        for c in range(GROUPS):
            lanes = pl.ds(c * TILE, TILE)
            parts = [prior_ref[NEAR + v, :, lanes]] + [ref[NEXT + c * FAR + v] for ref in (b1, b2, b3)]
            mixed = mix(coeffs[:MEMBERS], keep[:MEMBERS], parts)
            result[v, :, lanes] = mixed.astype(jnp.bfloat16)
        copies.append(pltpu.make_async_copy(result.at[v], out_ref.at[NEAR + v], sems.at[2 + v]))
        copies[-1].start()
    for copy in copies:
        copy.wait()


def analyse_far(me, weights, near, prior, bulk):
    return pl.pallas_call(
        far_kernel,
        out_shape=[
            jax.ShapeDtypeStruct((V, MEMBERS, GROUPS * TILE), jnp.bfloat16),
            jax.ShapeDtypeStruct((K, K), jnp.float32),
        ],
        in_specs=[SMEM] + [VMEM] * 6,
        out_specs=[ANY, ANY],
        scratch_shapes=[
            pltpu.VMEM((K, K), jnp.float32),
            pltpu.VMEM((FAR, MEMBERS, GROUPS * TILE), jnp.bfloat16),
            pltpu.SemaphoreType.DMA((2 + FAR,)),
        ],
        compiler_params=ROOM,
        name="analyse_far",
    )(me, weights, near, prior, *bulk)


def place_kernel(me_ref, c1, c2, c3, start_ref, out_ref, sems):
    del start_ref
    copies = []
    for s, chunk in enumerate((c1, c2, c3)):
        cells = pl.ds(pl.multiple_of(group_from(me_ref[0], s + 1) * TILE, TILE), TILE)
        copies.append(pltpu.make_async_copy(chunk, out_ref.at[pl.ds(0, NEAR), :, cells], sems.at[s]))
    for copy in copies:
        copy.start()
    for copy in copies:
        copy.wait()


def place(me, chunks, out):
    return pl.pallas_call(
        place_kernel,
        out_shape=jax.ShapeDtypeStruct(out.shape, out.dtype),
        in_specs=[SMEM] + [VMEM] * (GROUPS - 1) + [ANY],
        out_specs=ANY,
        scratch_shapes=[pltpu.SemaphoreType.DMA((GROUPS - 1,))],
        input_output_aliases={GROUPS: 0},
        compiler_params=ROOM,
        name="place",
    )(me, *chunks, out)


def ring(shift):
    return [(i, (i + shift) % GROUPS) for i in range(GROUPS)]


def scatter(chunks):
    return [lax.ppermute(chunk, "member", ring(s)) for s, chunk in enumerate(chunks, 1)]


def exchange(copies, axes):
    return lax.all_to_all(copies, axes, 0, 0, tiled=True)


def total(folded):
    copies = exchange(spread_sum(folded[None], PLANE, jnp.bfloat16), ("x", "z"))
    copies = exchange(spread_sum(copies, COLUMN), ("member", "core"))
    return spread_sum(copies, 1)[0]


def body(prior, readings, error_spread, mapping, slots):
    member = lax.axis_index("member").astype(jnp.int32)
    always = member < GROUPS
    me = (member + 1 - always.astype(jnp.int32)).reshape(1)
    prior = jnp.transpose(prior, (1, 0, 2))
    packed = pack(me, prior)
    observed = scatter(packed[1:])
    bulk = scatter(pack_bulk(me, prior, packed[0]))
    folded = observe(
        me, jnp.transpose(slots, (1, 2, 0))[0], [packed[0]] + observed, mapping[:, 0], readings, error_spread
    )
    folded = lax.cond(always, total, lambda x: x, folded)
    weights = transform(folded)
    near = analyse_near(me, weights, prior, observed, bulk)
    arrived = scatter(near[1:])
    out, weights = analyse_far(me, weights, near[0], prior, bulk)
    return (jnp.transpose(place(me, arrived, out), (1, 0, 2)), weights)


def solution(mesh):
    devices = mesh.devices.reshape(GROUPS, 4, 4, 2)
    axes = Mesh(devices, ("member", "x", "z", "core"))
    space = ("x", "z", "core")
    in_specs = (
        P("member", None, space),
        P(space, "member", None),
        P(space, "member", None),
        P(space, "member", None, None, None),
        P(space, "member", None),
    )
    out_specs = (P("member", None, space), P())
    return jax.shard_map(body, mesh=axes, in_specs=in_specs, out_specs=out_specs, check_vma=False)
```

```python
import functools

import jax
import jax.numpy as jnp
from jax import lax
from jax.experimental import pallas as pl
from jax.experimental.pallas import tpu as pltpu
from jax.sharding import Mesh
from jax.sharding import PartitionSpec as P

K = 96
V = 12
VOBS = 4
MEMBERS = 24
GROUPS = 4
TILE = 512
BLOCKS = 12
NNZ = 2
NS_ITERS = 4
HALF = K // 2
PLANE = 16
COLUMN = 8
NEAR = 7
COST = 40_000_000_000
FAR = V - NEAR
NEXT = NEAR - VOBS

EXACT = lax.Precision.HIGHEST
VMEM = pl.BlockSpec(memory_space=pltpu.VMEM)
SMEM = pl.BlockSpec(memory_space=pltpu.SMEM)
HBM = pl.BlockSpec(memory_space=pltpu.HBM)
ANY = pl.BlockSpec(memory_space=pl.ANY)
ROOM = pltpu.CompilerParams(vmem_limit_bytes=8 * 1024 * 1024)


def group_from(me, shift):
    return lax.rem(me + GROUPS - shift, GROUPS)


def group_to(me, shift):
    return lax.rem(me + shift, GROUPS)


def pack_kernel(me_ref, prior_ref, *refs):
    outs, sems = refs[:-1], refs[-1]
    copies = []
    for s in range(GROUPS):
        cells = pl.ds(pl.multiple_of(group_to(me_ref[0], s) * TILE, TILE), TILE)
        copies.append(pltpu.make_async_copy(prior_ref.at[pl.ds(0, VOBS), :, cells], outs[s], sems.at[s]))
    for copy in copies:
        copy.start()
    for copy in copies:
        copy.wait()


def pack(me, prior):
    return pl.pallas_call(
        pack_kernel,
        out_shape=[jax.ShapeDtypeStruct((VOBS, MEMBERS, TILE), prior.dtype)] * GROUPS,
        in_specs=[SMEM, HBM],
        out_specs=[VMEM] * GROUPS,
        scratch_shapes=[pltpu.SemaphoreType.DMA((GROUPS,))],
        compiler_params=ROOM,
        name="pack",
    )(me, prior)


def pack_bulk_kernel(me_ref, prior_ref, after_ref, *refs):
    del after_ref
    outs, sems = refs[:-1], refs[-1]
    copies = []
    for s, out in enumerate(outs, 1):
        cells = pl.ds(pl.multiple_of(group_to(me_ref[0], s) * TILE, TILE), TILE)
        copies.append((prior_ref.at[pl.ds(VOBS, NEXT), :, cells], out.at[pl.ds(0, NEXT)]))
        for c in range(GROUPS):
            source = prior_ref.at[pl.ds(NEAR, FAR), :, pl.ds(c * TILE, TILE)]
            copies.append((source, out.at[pl.ds(NEXT + c * FAR, FAR)]))
    copies = [pltpu.make_async_copy(*pair, sems.at[n]) for n, pair in enumerate(copies)]
    for copy in copies:
        copy.start()
    for copy in copies:
        copy.wait()


def pack_bulk(me, prior, after):
    return pl.pallas_call(
        pack_bulk_kernel,
        out_shape=[jax.ShapeDtypeStruct((NEXT + GROUPS * FAR, MEMBERS, TILE), prior.dtype)] * (GROUPS - 1),
        in_specs=[SMEM, ANY, ANY],
        out_specs=[HBM] * (GROUPS - 1),
        scratch_shapes=[pltpu.SemaphoreType.DMA(((GROUPS - 1) * (GROUPS + 1),))],
        compiler_params=ROOM,
        name="pack_bulk",
    )(me, prior, after)


def indices():
    row = lax.broadcasted_iota(jnp.int32, (HALF, 128), 0)
    lane = lax.broadcasted_iota(jnp.int32, (HALF, 128), 1)
    return row, lane


def fold(gram):
    row, lane = indices()
    top, low = gram[:HALF], gram[HALF:]
    second = pltpu.roll(low, 128 - HALF, 1)
    diagonal = jnp.sum(jnp.where(lane == row, second, 0.0), axis=1, keepdims=True)
    tail = jnp.sum(jnp.where(lane == HALF, second, 0.0), axis=1, keepdims=True)
    out = jnp.where((lane < HALF) & (lane > row), second, top)
    out = jnp.where(lane == K + 1, tail, out)
    return jnp.where(lane == K + 2, diagonal, out)


def unfold(folded):
    row, lane = indices()
    turned = jnp.concatenate([folded, jnp.zeros((128 - HALF, 128), jnp.float32)], axis=0).T
    flipped = turned[:HALF]
    first = jnp.where(lane <= row, folded, flipped)
    diagonal = folded[:, K + 2 : K + 3]
    second = jnp.where(lane < row, flipped, jnp.where(lane == row, diagonal, folded))
    top = jnp.where(lane < HALF, first, folded)
    low = jnp.where(lane < HALF, turned[HALF:K], pltpu.roll(second, HALF, 1))
    gram = jnp.concatenate([top, low], axis=0)[:, :K]
    projected = jnp.concatenate([folded[:, K : K + 1], folded[:, K + 1 : K + 2]], axis=0)
    return gram, projected


def split(a):
    high = a.astype(jnp.bfloat16)
    return high, (a - high.astype(jnp.float32)).astype(jnp.bfloat16)


def dot_rows(a, b):
    return lax.dot_general(a, b, (((1,), (1,)), ((), ())), preferred_element_type=jnp.float32)


def observe_kernel(me_ref, slots_ref, c0, c1, c2, c3, op_ref, y_ref, var_ref, out_ref, state):
    me = me_ref[0]
    for s, chunk in enumerate((c0, c1, c2, c3)):
        rows = pl.ds(pl.multiple_of(group_from(me, s) * MEMBERS, 8), MEMBERS)
        for v in range(VOBS):
            for c in range(TILE // 128):
                state[v * (TILE // 128) + c, rows, :] = chunk[v, :, c * 128 : (c + 1) * 128].astype(jnp.float32)
    spread, scaled = [], []
    projected = jnp.zeros((K, 128), jnp.float32)
    for b in range(BLOCKS):
        picked = [state[slots_ref[j, b]].astype(jnp.bfloat16) for j in range(NNZ)]
        mapping = jnp.concatenate([op_ref[b, j] for j in range(NNZ)], axis=1)
        pred = dot_rows(jnp.concatenate(picked, axis=1), mapping)
        mean = jnp.sum(pred, axis=0, keepdims=True) * (1.0 / K)
        spread.append(pred - mean)
        scaled.append(spread[-1] * (1.0 / var_ref[b]))
        projected += scaled[-1] * (y_ref[b] - mean)
    high, low = split(jnp.concatenate(scaled, axis=1))
    spread_high, spread_low = split(jnp.concatenate(spread, axis=1))
    both = dot_rows(jnp.concatenate([high, low], axis=0), spread_high)
    gram = both[:K] + both[K:] + dot_rows(high, spread_low)
    projected = jnp.sum(projected, axis=1, keepdims=True)
    out_ref[...] = fold(jnp.concatenate([gram, projected, jnp.zeros((K, 127 - K), jnp.float32)], axis=1))


def observe(me, slots, chunks, op, values, variances):
    return pl.pallas_call(
        observe_kernel,
        out_shape=jax.ShapeDtypeStruct((HALF, 128), jnp.float32),
        in_specs=[SMEM, SMEM] + [VMEM] * 7,
        out_specs=VMEM,
        scratch_shapes=[pltpu.VMEM((VOBS * TILE // 128, K, 128), jnp.float32)],
        compiler_params=ROOM,
        name="observe",
    )(me, slots, *chunks, op, values, variances)


def fine_dot(a, b):
    a_high, a_low = split(a)
    b_high, b_low = split(b)
    small = jnp.dot(a_high, b_low, preferred_element_type=jnp.float32)
    small += jnp.dot(a_low, b_high, preferred_element_type=jnp.float32)
    return small + jnp.dot(a_high, b_high, preferred_element_type=jnp.float32)


def narrow(folded):
    row, lane = indices()
    high = folded.astype(jnp.bfloat16).astype(jnp.float32)
    rest = folded - high
    low = pltpu.roll(rest, 3, 1)
    diagonal = jnp.sum(jnp.where(lane == row, rest, 0.0), axis=1, keepdims=True)
    out = jnp.where((lane >= K + 3) & (lane < K + 6), low, high)
    return jnp.where(lane == K + 6, diagonal, out).astype(jnp.bfloat16)


def widen(total):
    row, lane = indices()
    out = jnp.where((lane >= K) & (lane < K + 3), total + pltpu.roll(total, 125, 1), total)
    return jnp.where(lane == row, out + total[:, K + 6 : K + 7], out)


def spread_kernel(parts_ref, out_ref):
    total = parts_ref[0].astype(jnp.float32)
    for part in range(1, parts_ref.shape[0]):
        total = total + parts_ref[part].astype(jnp.float32)
    if parts_ref.dtype == jnp.bfloat16:
        total = widen(total)
    if out_ref.dtype == jnp.bfloat16:
        total = narrow(total)
    for copy in range(out_ref.shape[0]):
        out_ref[copy] = total


def spread_sum(parts, copies, dtype=jnp.float32):
    return pl.pallas_call(
        spread_kernel,
        out_shape=jax.ShapeDtypeStruct((copies, HALF, 128), dtype),
        in_specs=[VMEM],
        out_specs=VMEM,
        compiler_params=ROOM,
        name="spread_sum",
    )(parts)


def transform_kernel(parts_ref, weights_ref):
    folded = parts_ref[...]
    gram, projected = unfold(folded)
    row = lax.broadcasted_iota(jnp.int32, (K, K), 0)
    col = lax.broadcasted_iota(jnp.int32, (K, K), 1)
    eye = jnp.where(row == col, 1.0, 0.0).astype(jnp.float32)
    system = gram + (K - 1.0) * eye
    frob = jnp.sqrt(jnp.sum(system * system, keepdims=True))
    root = system / frob
    inverse = None
    for step in range(NS_ITERS):
        product = root if inverse is None else fine_dot(inverse, root)
        factor = 1.5 * eye - 0.5 * product
        if step < NS_ITERS - 1:
            root = fine_dot(root, factor)
        inverse = factor if inverse is None else fine_dot(factor, inverse)
    inverse_root = inverse / jnp.sqrt(frob)
    halfway = jnp.sum(inverse_root * projected, axis=0, keepdims=True)
    mean_shift = jnp.sum(inverse_root * halfway, axis=1, keepdims=True)
    weights_ref[...] = mean_shift + (K - 1.0) ** 0.5 * inverse_root


def transform(parts):
    return pl.pallas_call(
        transform_kernel,
        out_shape=jax.ShapeDtypeStruct((K, K), jnp.float32),
        in_specs=[VMEM],
        out_specs=VMEM,
        compiler_params=ROOM,
        cost_estimate=pl.CostEstimate(flops=COST, bytes_accessed=0, transcendentals=0),
        name="transform",
    )(parts)


def regroup(x, me, which):
    return jnp.concatenate(
        [x[pl.ds(pl.multiple_of(which(me, s) * MEMBERS, 8), MEMBERS), :] for s in range(GROUPS)], axis=0
    )


def coefficients(me, w_ref, turned):
    turned[...] = regroup(w_ref, me, group_from).T
    coeffs = regroup(turned, me, group_to).astype(jnp.bfloat16)
    return coeffs, 1.0 - jnp.sum(coeffs.astype(jnp.float32), axis=1, keepdims=True)


def mix(coeffs, keep, parts):
    stacked = jnp.concatenate([part.astype(jnp.float32) for part in parts], axis=0)
    center = jnp.sum(stacked, axis=0, keepdims=True) * (1.0 / K)
    mixed = jnp.dot(coeffs, stacked.astype(jnp.bfloat16), preferred_element_type=jnp.float32)
    return mixed + keep * center


def near_kernel(me_ref, w_ref, prior_ref, o1, o2, o3, b1, b2, b3, a0, a1, a2, a3, turned):
    coeffs, keep = coefficients(me_ref[0], w_ref, turned)
    cells = pl.ds(pl.multiple_of(me_ref[0] * TILE, TILE), TILE)
    for v in range(NEAR):
        parts = [ref[v] for ref in (o1, o2, o3)] if v < VOBS else [ref[v - VOBS] for ref in (b1, b2, b3)]
        parts = [prior_ref[v, :, cells]] + parts
        mixed = mix(coeffs, keep, parts)
        for g, out in enumerate((a0, a1, a2, a3)):
            out[v] = mixed[g * MEMBERS : (g + 1) * MEMBERS].astype(jnp.bfloat16)


def analyse_near(me, weights, prior, observed, bulk):
    return pl.pallas_call(
        near_kernel,
        out_shape=[jax.ShapeDtypeStruct((NEAR, MEMBERS, TILE), jnp.bfloat16)] * GROUPS,
        in_specs=[SMEM] + [VMEM] * 8,
        out_specs=[VMEM] * GROUPS,
        scratch_shapes=[pltpu.VMEM((K, K), jnp.float32)],
        compiler_params=ROOM,
        name="analyse_near",
    )(me, weights, prior, *observed, *bulk)


def far_kernel(me_ref, w_ref, near_ref, prior_ref, b1, b2, b3, out_ref, weights_ref, turned, result, sems):
    me = me_ref[0]
    cells = pl.ds(pl.multiple_of(me * TILE, TILE), TILE)
    copies = [
        pltpu.make_async_copy(near_ref, out_ref.at[pl.ds(0, NEAR), :, cells], sems.at[0]),
        pltpu.make_async_copy(w_ref, weights_ref, sems.at[1]),
    ]
    for copy in copies:
        copy.start()
    coeffs, keep = coefficients(me, w_ref, turned)
    for v in range(FAR):
        for c in range(GROUPS):
            lanes = pl.ds(c * TILE, TILE)
            parts = [prior_ref[NEAR + v, :, lanes]] + [ref[NEXT + c * FAR + v] for ref in (b1, b2, b3)]
            mixed = mix(coeffs[:MEMBERS], keep[:MEMBERS], parts)
            result[v, :, lanes] = mixed.astype(jnp.bfloat16)
        copies.append(pltpu.make_async_copy(result.at[v], out_ref.at[NEAR + v], sems.at[2 + v]))
        copies[-1].start()
    for copy in copies:
        copy.wait()


def analyse_far(me, weights, near, prior, bulk):
    return pl.pallas_call(
        far_kernel,
        out_shape=[
            jax.ShapeDtypeStruct((V, MEMBERS, GROUPS * TILE), jnp.bfloat16),
            jax.ShapeDtypeStruct((K, K), jnp.float32),
        ],
        in_specs=[SMEM] + [VMEM] * 6,
        out_specs=[ANY, ANY],
        scratch_shapes=[
            pltpu.VMEM((K, K), jnp.float32),
            pltpu.VMEM((FAR, MEMBERS, GROUPS * TILE), jnp.bfloat16),
            pltpu.SemaphoreType.DMA((2 + FAR,)),
        ],
        compiler_params=ROOM,
        name="analyse_far",
    )(me, weights, near, prior, *bulk)


def place_kernel(me_ref, c1, c2, c3, start_ref, out_ref, sems):
    del start_ref
    copies = []
    for s, chunk in enumerate((c1, c2, c3)):
        cells = pl.ds(pl.multiple_of(group_from(me_ref[0], s + 1) * TILE, TILE), TILE)
        copies.append(pltpu.make_async_copy(chunk, out_ref.at[pl.ds(0, NEAR), :, cells], sems.at[s]))
    for copy in copies:
        copy.start()
    for copy in copies:
        copy.wait()


def place(me, chunks, out):
    return pl.pallas_call(
        place_kernel,
        out_shape=jax.ShapeDtypeStruct(out.shape, out.dtype),
        in_specs=[SMEM] + [VMEM] * (GROUPS - 1) + [ANY],
        out_specs=ANY,
        scratch_shapes=[pltpu.SemaphoreType.DMA((GROUPS - 1,))],
        input_output_aliases={GROUPS: 0},
        compiler_params=ROOM,
        name="place",
    )(me, *chunks, out)


def ring(shift):
    return [(i, (i + shift) % GROUPS) for i in range(GROUPS)]


def scatter(chunks):
    return [lax.ppermute(chunk, "member", ring(s)) for s, chunk in enumerate(chunks, 1)]


def exchange(copies, axes):
    return lax.all_to_all(copies, axes, 0, 0, tiled=True)


def total(folded):
    copies = exchange(spread_sum(folded[None], PLANE, jnp.bfloat16), ("x", "z"))
    copies = exchange(spread_sum(copies, COLUMN, jnp.bfloat16), ("member", "core"))
    return spread_sum(copies, 1)[0]


def body(prior, readings, error_spread, mapping, slots):
    member = lax.axis_index("member").astype(jnp.int32)
    always = member < GROUPS
    me = (member + 1 - always.astype(jnp.int32)).reshape(1)
    prior = jnp.transpose(prior, (1, 0, 2))
    packed = pack(me, prior)
    observed = scatter(packed[1:])
    bulk = scatter(pack_bulk(me, prior, packed[0]))
    folded = observe(
        me, jnp.transpose(slots, (1, 2, 0))[0], [packed[0]] + observed, mapping[:, 0], readings, error_spread
    )
    folded = lax.cond(always, total, lambda x: x, folded)
    weights = transform(folded)
    near = analyse_near(me, weights, prior, observed, bulk)
    arrived = scatter(near[1:])
    out, weights = analyse_far(me, weights, near[0], prior, bulk)
    return (jnp.transpose(place(me, arrived, out), (1, 0, 2)), weights)


def solution(mesh):
    devices = mesh.devices.reshape(GROUPS, 4, 4, 2)
    axes = Mesh(devices, ("member", "x", "z", "core"))
    space = ("x", "z", "core")
    in_specs = (
        P("member", None, space),
        P(space, "member", None),
        P(space, "member", None),
        P(space, "member", None, None, None),
        P(space, "member", None),
    )
    out_specs = (P("member", None, space), P())
    return jax.shard_map(body, mesh=axes, in_specs=in_specs, out_specs=out_specs, check_vma=False)
```

```python
import functools

import jax
import jax.numpy as jnp
from jax import lax
from jax.experimental import pallas as pl
from jax.experimental.pallas import tpu as pltpu
from jax.sharding import Mesh
from jax.sharding import PartitionSpec as P

K = 96
V = 12
VOBS = 4
MEMBERS = 24
GROUPS = 4
TILE = 512
BLOCKS = 12
NNZ = 2
NS_ITERS = 4
HALF = K // 2
PLANE = 16
COLUMN = 8
NEAR = 7
COST = 40_000_000_000
FAR = V - NEAR
NEXT = NEAR - VOBS

EXACT = lax.Precision.HIGHEST
VMEM = pl.BlockSpec(memory_space=pltpu.VMEM)
SMEM = pl.BlockSpec(memory_space=pltpu.SMEM)
HBM = pl.BlockSpec(memory_space=pltpu.HBM)
ANY = pl.BlockSpec(memory_space=pl.ANY)
ROOM = pltpu.CompilerParams(vmem_limit_bytes=8 * 1024 * 1024)


def group_from(me, shift):
    return lax.rem(me + GROUPS - shift, GROUPS)


def group_to(me, shift):
    return lax.rem(me + shift, GROUPS)


def pack_kernel(me_ref, prior_ref, *refs):
    outs, sems = refs[:-1], refs[-1]
    copies = []
    for s in range(GROUPS):
        cells = pl.ds(pl.multiple_of(group_to(me_ref[0], s) * TILE, TILE), TILE)
        copies.append(pltpu.make_async_copy(prior_ref.at[pl.ds(0, VOBS), :, cells], outs[s], sems.at[s]))
    for copy in copies:
        copy.start()
    for copy in copies:
        copy.wait()


def pack(me, prior):
    return pl.pallas_call(
        pack_kernel,
        out_shape=[jax.ShapeDtypeStruct((VOBS, MEMBERS, TILE), prior.dtype)] * GROUPS,
        in_specs=[SMEM, HBM],
        out_specs=[VMEM] * GROUPS,
        scratch_shapes=[pltpu.SemaphoreType.DMA((GROUPS,))],
        compiler_params=ROOM,
        name="pack",
    )(me, prior)


def pack_bulk_kernel(me_ref, prior_ref, after_ref, *refs):
    del after_ref
    outs, sems = refs[:-1], refs[-1]
    copies = []
    for s, out in enumerate(outs, 1):
        cells = pl.ds(pl.multiple_of(group_to(me_ref[0], s) * TILE, TILE), TILE)
        copies.append((prior_ref.at[pl.ds(VOBS, NEXT), :, cells], out.at[pl.ds(0, NEXT)]))
        for c in range(GROUPS):
            source = prior_ref.at[pl.ds(NEAR, FAR), :, pl.ds(c * TILE, TILE)]
            copies.append((source, out.at[pl.ds(NEXT + c * FAR, FAR)]))
    copies = [pltpu.make_async_copy(*pair, sems.at[n]) for n, pair in enumerate(copies)]
    for copy in copies:
        copy.start()
    for copy in copies:
        copy.wait()


def pack_bulk(me, prior, after):
    return pl.pallas_call(
        pack_bulk_kernel,
        out_shape=[jax.ShapeDtypeStruct((NEXT + GROUPS * FAR, MEMBERS, TILE), prior.dtype)] * (GROUPS - 1),
        in_specs=[SMEM, ANY, ANY],
        out_specs=[HBM] * (GROUPS - 1),
        scratch_shapes=[pltpu.SemaphoreType.DMA(((GROUPS - 1) * (GROUPS + 1),))],
        compiler_params=ROOM,
        name="pack_bulk",
    )(me, prior, after)


def indices():
    row = lax.broadcasted_iota(jnp.int32, (HALF, 128), 0)
    lane = lax.broadcasted_iota(jnp.int32, (HALF, 128), 1)
    return row, lane


def fold(gram):
    row, lane = indices()
    top, low = gram[:HALF], gram[HALF:]
    second = pltpu.roll(low, 128 - HALF, 1)
    diagonal = jnp.sum(jnp.where(lane == row, second, 0.0), axis=1, keepdims=True)
    tail = jnp.sum(jnp.where(lane == HALF, second, 0.0), axis=1, keepdims=True)
    out = jnp.where((lane < HALF) & (lane > row), second, top)
    out = jnp.where(lane == K + 1, tail, out)
    return jnp.where(lane == K + 2, diagonal, out)


def unfold(folded):
    row, lane = indices()
    turned = jnp.concatenate([folded, jnp.zeros((128 - HALF, 128), jnp.float32)], axis=0).T
    flipped = turned[:HALF]
    first = jnp.where(lane <= row, folded, flipped)
    diagonal = folded[:, K + 2 : K + 3]
    second = jnp.where(lane < row, flipped, jnp.where(lane == row, diagonal, folded))
    top = jnp.where(lane < HALF, first, folded)
    low = jnp.where(lane < HALF, turned[HALF:K], pltpu.roll(second, HALF, 1))
    gram = jnp.concatenate([top, low], axis=0)[:, :K]
    projected = jnp.concatenate([folded[:, K : K + 1], folded[:, K + 1 : K + 2]], axis=0)
    return gram, projected


def split(a):
    high = a.astype(jnp.bfloat16)
    return high, (a - high.astype(jnp.float32)).astype(jnp.bfloat16)


def dot_rows(a, b):
    return lax.dot_general(a, b, (((1,), (1,)), ((), ())), preferred_element_type=jnp.float32)


def observe_kernel(me_ref, slots_ref, c0, c1, c2, c3, op_ref, y_ref, var_ref, out_ref, state):
    me = me_ref[0]
    for s, chunk in enumerate((c0, c1, c2, c3)):
        rows = pl.ds(pl.multiple_of(group_from(me, s) * MEMBERS, 8), MEMBERS)
        for v in range(VOBS):
            for c in range(TILE // 128):
                state[v * (TILE // 128) + c, rows, :] = chunk[v, :, c * 128 : (c + 1) * 128].astype(jnp.float32)
    spread, scaled = [], []
    projected = jnp.zeros((K, 128), jnp.float32)
    for b in range(BLOCKS):
        picked = [state[slots_ref[j, b]].astype(jnp.bfloat16) for j in range(NNZ)]
        mapping = jnp.concatenate([op_ref[b, j] for j in range(NNZ)], axis=1)
        pred = dot_rows(jnp.concatenate(picked, axis=1), mapping)
        mean = jnp.sum(pred, axis=0, keepdims=True) * (1.0 / K)
        spread.append(pred - mean)
        scaled.append(spread[-1] * (1.0 / var_ref[b]))
        projected += scaled[-1] * (y_ref[b] - mean)
    high, low = split(jnp.concatenate(scaled, axis=1))
    spread_high, spread_low = split(jnp.concatenate(spread, axis=1))
    both = dot_rows(jnp.concatenate([high, low], axis=0), spread_high)
    gram = both[:K] + both[K:] + dot_rows(high, spread_low)
    projected = jnp.sum(projected, axis=1, keepdims=True)
    folded = narrow(fold(jnp.concatenate([gram, projected, jnp.zeros((K, 127 - K), jnp.float32)], axis=1)))
    for copy in range(PLANE):
        out_ref[copy] = folded


def observe(me, slots, chunks, op, values, variances):
    return pl.pallas_call(
        observe_kernel,
        out_shape=jax.ShapeDtypeStruct((PLANE, HALF, 128), jnp.bfloat16),
        in_specs=[SMEM, SMEM] + [VMEM] * 7,
        out_specs=VMEM,
        scratch_shapes=[pltpu.VMEM((VOBS * TILE // 128, K, 128), jnp.float32)],
        compiler_params=ROOM,
        name="observe",
    )(me, slots, *chunks, op, values, variances)


def fine_dot(a, b):
    a_high, a_low = split(a)
    b_high, b_low = split(b)
    small = jnp.dot(a_high, b_low, preferred_element_type=jnp.float32)
    small += jnp.dot(a_low, b_high, preferred_element_type=jnp.float32)
    return small + jnp.dot(a_high, b_high, preferred_element_type=jnp.float32)


def narrow(folded):
    row, lane = indices()
    high = folded.astype(jnp.bfloat16).astype(jnp.float32)
    rest = folded - high
    low = pltpu.roll(rest, 3, 1)
    diagonal = jnp.sum(jnp.where(lane == row, rest, 0.0), axis=1, keepdims=True)
    out = jnp.where((lane >= K + 3) & (lane < K + 6), low, high)
    return jnp.where(lane == K + 6, diagonal, out).astype(jnp.bfloat16)


def widen(total):
    row, lane = indices()
    out = jnp.where((lane >= K) & (lane < K + 3), total + pltpu.roll(total, 125, 1), total)
    return jnp.where(lane == row, out + total[:, K + 6 : K + 7], out)


def sum_parts(parts_ref):
    total = parts_ref[0].astype(jnp.float32)
    for part in range(1, parts_ref.shape[0]):
        total = total + parts_ref[part].astype(jnp.float32)
    return widen(total) if parts_ref.dtype == jnp.bfloat16 else total


def spread_kernel(parts_ref, out_ref):
    total = sum_parts(parts_ref)
    if out_ref.dtype == jnp.bfloat16:
        total = narrow(total)
    for copy in range(out_ref.shape[0]):
        out_ref[copy] = total


def spread_sum(parts, copies, dtype=jnp.float32):
    return pl.pallas_call(
        spread_kernel,
        out_shape=jax.ShapeDtypeStruct((copies, HALF, 128), dtype),
        in_specs=[VMEM],
        out_specs=VMEM,
        compiler_params=ROOM,
        name="spread_sum",
    )(parts)


def transform_kernel(parts_ref, weights_ref):
    folded = sum_parts(parts_ref)
    gram, projected = unfold(folded)
    row = lax.broadcasted_iota(jnp.int32, (K, K), 0)
    col = lax.broadcasted_iota(jnp.int32, (K, K), 1)
    eye = jnp.where(row == col, 1.0, 0.0).astype(jnp.float32)
    system = gram + (K - 1.0) * eye
    frob = jnp.sqrt(jnp.sum(system * system, keepdims=True))
    root = system / frob
    inverse = None
    for step in range(NS_ITERS):
        product = root if inverse is None else fine_dot(inverse, root)
        factor = 1.5 * eye - 0.5 * product
        if step < NS_ITERS - 1:
            root = fine_dot(root, factor)
        inverse = factor if inverse is None else fine_dot(factor, inverse)
    inverse_root = inverse / jnp.sqrt(frob)
    halfway = jnp.sum(inverse_root * projected, axis=0, keepdims=True)
    mean_shift = jnp.sum(inverse_root * halfway, axis=1, keepdims=True)
    weights_ref[...] = mean_shift + (K - 1.0) ** 0.5 * inverse_root


def transform(parts):
    return pl.pallas_call(
        transform_kernel,
        out_shape=jax.ShapeDtypeStruct((K, K), jnp.float32),
        in_specs=[VMEM],
        out_specs=VMEM,
        compiler_params=ROOM,
        cost_estimate=pl.CostEstimate(flops=COST, bytes_accessed=0, transcendentals=0),
        name="transform",
    )(parts)


def regroup(x, me, which):
    return jnp.concatenate(
        [x[pl.ds(pl.multiple_of(which(me, s) * MEMBERS, 8), MEMBERS), :] for s in range(GROUPS)], axis=0
    )


def coefficients(me, w_ref, turned):
    turned[...] = regroup(w_ref, me, group_from).T
    coeffs = regroup(turned, me, group_to).astype(jnp.bfloat16)
    return coeffs, 1.0 - jnp.sum(coeffs.astype(jnp.float32), axis=1, keepdims=True)


def mix(coeffs, keep, parts):
    stacked = jnp.concatenate([part.astype(jnp.float32) for part in parts], axis=0)
    center = jnp.sum(stacked, axis=0, keepdims=True) * (1.0 / K)
    mixed = jnp.dot(coeffs, stacked.astype(jnp.bfloat16), preferred_element_type=jnp.float32)
    return mixed + keep * center


def near_kernel(me_ref, w_ref, prior_ref, o1, o2, o3, b1, b2, b3, a0, a1, a2, a3, turned):
    coeffs, keep = coefficients(me_ref[0], w_ref, turned)
    cells = pl.ds(pl.multiple_of(me_ref[0] * TILE, TILE), TILE)
    for v in range(NEAR):
        parts = [ref[v] for ref in (o1, o2, o3)] if v < VOBS else [ref[v - VOBS] for ref in (b1, b2, b3)]
        parts = [prior_ref[v, :, cells]] + parts
        mixed = mix(coeffs, keep, parts)
        for g, out in enumerate((a0, a1, a2, a3)):
            out[v] = mixed[g * MEMBERS : (g + 1) * MEMBERS].astype(jnp.bfloat16)


def analyse_near(me, weights, prior, observed, bulk):
    return pl.pallas_call(
        near_kernel,
        out_shape=[jax.ShapeDtypeStruct((NEAR, MEMBERS, TILE), jnp.bfloat16)] * GROUPS,
        in_specs=[SMEM] + [VMEM] * 8,
        out_specs=[VMEM] * GROUPS,
        scratch_shapes=[pltpu.VMEM((K, K), jnp.float32)],
        compiler_params=ROOM,
        name="analyse_near",
    )(me, weights, prior, *observed, *bulk)


def far_kernel(me_ref, w_ref, near_ref, prior_ref, b1, b2, b3, out_ref, weights_ref, turned, result, sems):
    me = me_ref[0]
    cells = pl.ds(pl.multiple_of(me * TILE, TILE), TILE)
    copies = [
        pltpu.make_async_copy(near_ref, out_ref.at[pl.ds(0, NEAR), :, cells], sems.at[0]),
        pltpu.make_async_copy(w_ref, weights_ref, sems.at[1]),
    ]
    for copy in copies:
        copy.start()
    coeffs, keep = coefficients(me, w_ref, turned)
    for v in range(FAR):
        for c in range(GROUPS):
            lanes = pl.ds(c * TILE, TILE)
            parts = [prior_ref[NEAR + v, :, lanes]] + [ref[NEXT + c * FAR + v] for ref in (b1, b2, b3)]
            mixed = mix(coeffs[:MEMBERS], keep[:MEMBERS], parts)
            result[v, :, lanes] = mixed.astype(jnp.bfloat16)
        copies.append(pltpu.make_async_copy(result.at[v], out_ref.at[NEAR + v], sems.at[2 + v]))
        copies[-1].start()
    for copy in copies:
        copy.wait()


def analyse_far(me, weights, near, prior, bulk):
    return pl.pallas_call(
        far_kernel,
        out_shape=[
            jax.ShapeDtypeStruct((V, MEMBERS, GROUPS * TILE), jnp.bfloat16),
            jax.ShapeDtypeStruct((K, K), jnp.float32),
        ],
        in_specs=[SMEM] + [VMEM] * 6,
        out_specs=[ANY, ANY],
        scratch_shapes=[
            pltpu.VMEM((K, K), jnp.float32),
            pltpu.VMEM((FAR, MEMBERS, GROUPS * TILE), jnp.bfloat16),
            pltpu.SemaphoreType.DMA((2 + FAR,)),
        ],
        compiler_params=ROOM,
        name="analyse_far",
    )(me, weights, near, prior, *bulk)


def place_kernel(me_ref, c1, c2, c3, start_ref, out_ref, sems):
    del start_ref
    copies = []
    for s, chunk in enumerate((c1, c2, c3)):
        cells = pl.ds(pl.multiple_of(group_from(me_ref[0], s + 1) * TILE, TILE), TILE)
        copies.append(pltpu.make_async_copy(chunk, out_ref.at[pl.ds(0, NEAR), :, cells], sems.at[s]))
    for copy in copies:
        copy.start()
    for copy in copies:
        copy.wait()


def place(me, chunks, out):
    return pl.pallas_call(
        place_kernel,
        out_shape=jax.ShapeDtypeStruct(out.shape, out.dtype),
        in_specs=[SMEM] + [VMEM] * (GROUPS - 1) + [ANY],
        out_specs=ANY,
        scratch_shapes=[pltpu.SemaphoreType.DMA((GROUPS - 1,))],
        input_output_aliases={GROUPS: 0},
        compiler_params=ROOM,
        name="place",
    )(me, *chunks, out)


def ring(shift):
    return [(i, (i + shift) % GROUPS) for i in range(GROUPS)]


def scatter(chunks):
    return [lax.ppermute(chunk, "member", ring(s)) for s, chunk in enumerate(chunks, 1)]


def exchange(copies, axes):
    return lax.all_to_all(copies, axes, 0, 0, tiled=True)


def total(copies):
    copies = exchange(copies, ("x", "z"))
    copies = exchange(spread_sum(copies, COLUMN, jnp.bfloat16), ("member", "core"))
    return copies


def body(prior, readings, error_spread, mapping, slots):
    member = lax.axis_index("member").astype(jnp.int32)
    always = member < GROUPS
    me = (member + 1 - always.astype(jnp.int32)).reshape(1)
    prior = jnp.transpose(prior, (1, 0, 2))
    packed = pack(me, prior)
    observed = scatter(packed[1:])
    bulk = scatter(pack_bulk(me, prior, packed[0]))
    folded = observe(
        me, jnp.transpose(slots, (1, 2, 0))[0], [packed[0]] + observed, mapping[:, 0], readings, error_spread
    )
    folded = lax.cond(
        always, total, lambda x: jnp.zeros((COLUMN, HALF, 128), jnp.bfloat16), folded
    )
    weights = transform(folded)
    near = analyse_near(me, weights, prior, observed, bulk)
    arrived = scatter(near[1:])
    out, weights = analyse_far(me, weights, near[0], prior, bulk)
    return (jnp.transpose(place(me, arrived, out), (1, 0, 2)), weights)


def solution(mesh):
    devices = mesh.devices.reshape(GROUPS, 4, 4, 2)
    axes = Mesh(devices, ("member", "x", "z", "core"))
    space = ("x", "z", "core")
    in_specs = (
        P("member", None, space),
        P(space, "member", None),
        P(space, "member", None),
        P(space, "member", None, None, None),
        P(space, "member", None),
    )
    out_specs = (P("member", None, space), P())
    return jax.shard_map(body, mesh=axes, in_specs=in_specs, out_specs=out_specs, check_vma=False)
```

```python
import functools

import jax
import jax.numpy as jnp
from jax import lax
from jax.experimental import pallas as pl
from jax.experimental.pallas import tpu as pltpu
from jax.sharding import Mesh
from jax.sharding import PartitionSpec as P

K = 96
V = 12
VOBS = 4
MEMBERS = 24
GROUPS = 4
TILE = 512
BLOCKS = 12
NNZ = 2
NS_ITERS = 4
HALF = K // 2
PLANE = 16
COLUMN = 8
NEAR = 7
COST = 40_000_000_000
FAR = V - NEAR
NEXT = NEAR - VOBS

EXACT = lax.Precision.HIGHEST
VMEM = pl.BlockSpec(memory_space=pltpu.VMEM)
SMEM = pl.BlockSpec(memory_space=pltpu.SMEM)
HBM = pl.BlockSpec(memory_space=pltpu.HBM)
ANY = pl.BlockSpec(memory_space=pl.ANY)
ROOM = pltpu.CompilerParams(vmem_limit_bytes=8 * 1024 * 1024)


def group_from(me, shift):
    return lax.rem(me + GROUPS - shift, GROUPS)


def group_to(me, shift):
    return lax.rem(me + shift, GROUPS)


def pack_kernel(me_ref, prior_ref, *refs):
    outs, sems = refs[:-1], refs[-1]
    copies = []
    for s in range(GROUPS):
        cells = pl.ds(pl.multiple_of(group_to(me_ref[0], s) * TILE, TILE), TILE)
        copies.append(pltpu.make_async_copy(prior_ref.at[pl.ds(0, VOBS), :, cells], outs[s], sems.at[s]))
    for copy in copies:
        copy.start()
    for copy in copies:
        copy.wait()


def pack(me, prior):
    return pl.pallas_call(
        pack_kernel,
        out_shape=[jax.ShapeDtypeStruct((VOBS, MEMBERS, TILE), prior.dtype)] * GROUPS,
        in_specs=[SMEM, HBM],
        out_specs=[VMEM] * GROUPS,
        scratch_shapes=[pltpu.SemaphoreType.DMA((GROUPS,))],
        compiler_params=ROOM,
        name="pack",
    )(me, prior)


def pack_bulk_kernel(me_ref, prior_ref, after_ref, *refs):
    del after_ref
    outs, sems = refs[:-1], refs[-1]
    copies = []
    for s, out in enumerate(outs, 1):
        cells = pl.ds(pl.multiple_of(group_to(me_ref[0], s) * TILE, TILE), TILE)
        copies.append((prior_ref.at[pl.ds(VOBS, NEXT), :, cells], out.at[pl.ds(0, NEXT)]))
        for c in range(GROUPS):
            source = prior_ref.at[pl.ds(NEAR, FAR), :, pl.ds(c * TILE, TILE)]
            copies.append((source, out.at[pl.ds(NEXT + c * FAR, FAR)]))
    copies = [pltpu.make_async_copy(*pair, sems.at[n]) for n, pair in enumerate(copies)]
    for copy in copies:
        copy.start()
    for copy in copies:
        copy.wait()


def pack_bulk(me, prior, after):
    return pl.pallas_call(
        pack_bulk_kernel,
        out_shape=[jax.ShapeDtypeStruct((NEXT + GROUPS * FAR, MEMBERS, TILE), prior.dtype)] * (GROUPS - 1),
        in_specs=[SMEM, ANY, ANY],
        out_specs=[HBM] * (GROUPS - 1),
        scratch_shapes=[pltpu.SemaphoreType.DMA(((GROUPS - 1) * (GROUPS + 1),))],
        compiler_params=ROOM,
        name="pack_bulk",
    )(me, prior, after)


def indices():
    row = lax.broadcasted_iota(jnp.int32, (HALF, 128), 0)
    lane = lax.broadcasted_iota(jnp.int32, (HALF, 128), 1)
    return row, lane


def fold(gram):
    row, lane = indices()
    top, low = gram[:HALF], gram[HALF:]
    second = pltpu.roll(low, 128 - HALF, 1)
    diagonal = jnp.sum(jnp.where(lane == row, second, 0.0), axis=1, keepdims=True)
    tail = jnp.sum(jnp.where(lane == HALF, second, 0.0), axis=1, keepdims=True)
    out = jnp.where((lane < HALF) & (lane > row), second, top)
    out = jnp.where(lane == K + 1, tail, out)
    return jnp.where(lane == K + 2, diagonal, out)


def unfold(folded):
    row, lane = indices()
    turned = jnp.concatenate([folded, jnp.zeros((128 - HALF, 128), jnp.float32)], axis=0).T
    flipped = turned[:HALF]
    first = jnp.where(lane <= row, folded, flipped)
    diagonal = folded[:, K + 2 : K + 3]
    second = jnp.where(lane < row, flipped, jnp.where(lane == row, diagonal, folded))
    top = jnp.where(lane < HALF, first, folded)
    low = jnp.where(lane < HALF, turned[HALF:K], pltpu.roll(second, HALF, 1))
    gram = jnp.concatenate([top, low], axis=0)[:, :K]
    projected = jnp.concatenate([folded[:, K : K + 1], folded[:, K + 1 : K + 2]], axis=0)
    return gram, projected


def split(a):
    high = a.astype(jnp.bfloat16)
    return high, (a - high.astype(jnp.float32)).astype(jnp.bfloat16)


def dot_rows(a, b):
    return lax.dot_general(a, b, (((1,), (1,)), ((), ())), preferred_element_type=jnp.float32)


def observe_kernel(me_ref, slots_ref, c0, c1, c2, c3, op_ref, y_ref, var_ref, out_ref, state):
    me = me_ref[0]
    for s, chunk in enumerate((c0, c1, c2, c3)):
        rows = pl.ds(pl.multiple_of(group_from(me, s) * MEMBERS, 8), MEMBERS)
        for v in range(VOBS):
            for c in range(TILE // 128):
                state[v * (TILE // 128) + c, rows, :] = chunk[v, :, c * 128 : (c + 1) * 128].astype(jnp.float32)
    spread, scaled = [], []
    projected = jnp.zeros((K, 128), jnp.float32)
    for b in range(BLOCKS):
        picked = [state[slots_ref[j, b]].astype(jnp.bfloat16) for j in range(NNZ)]
        mapping = jnp.concatenate([op_ref[b, j] for j in range(NNZ)], axis=1)
        pred = dot_rows(jnp.concatenate(picked, axis=1), mapping)
        mean = jnp.sum(pred, axis=0, keepdims=True) * (1.0 / K)
        spread.append(pred - mean)
        scaled.append(spread[-1] * (1.0 / var_ref[b]))
        projected += scaled[-1] * (y_ref[b] - mean)
    high, low = split(jnp.concatenate(scaled, axis=1))
    spread_high, spread_low = split(jnp.concatenate(spread, axis=1))
    both = dot_rows(jnp.concatenate([high, low], axis=0), spread_high)
    gram = both[:K] + both[K:] + dot_rows(high, spread_low)
    projected = jnp.sum(projected, axis=1, keepdims=True)
    out_ref[...] = fold(jnp.concatenate([gram, projected, jnp.zeros((K, 127 - K), jnp.float32)], axis=1))


def observe(me, slots, chunks, op, values, variances):
    return pl.pallas_call(
        observe_kernel,
        out_shape=jax.ShapeDtypeStruct((HALF, 128), jnp.float32),
        in_specs=[SMEM, SMEM] + [VMEM] * 7,
        out_specs=VMEM,
        scratch_shapes=[pltpu.VMEM((VOBS * TILE // 128, K, 128), jnp.float32)],
        compiler_params=ROOM,
        name="observe",
    )(me, slots, *chunks, op, values, variances)


def fine_dot(a, b):
    a_high, a_low = split(a)
    b_high, b_low = split(b)
    small = jnp.dot(a_high, b_low, preferred_element_type=jnp.float32)
    small += jnp.dot(a_low, b_high, preferred_element_type=jnp.float32)
    return small + jnp.dot(a_high, b_high, preferred_element_type=jnp.float32)


def narrow(folded):
    row, lane = indices()
    high = folded.astype(jnp.bfloat16).astype(jnp.float32)
    rest = folded - high
    low = pltpu.roll(rest, 3, 1)
    diagonal = jnp.sum(jnp.where(lane == row, rest, 0.0), axis=1, keepdims=True)
    out = jnp.where((lane >= K + 3) & (lane < K + 6), low, high)
    return jnp.where(lane == K + 6, diagonal, out).astype(jnp.bfloat16)


def widen(total):
    row, lane = indices()
    out = jnp.where((lane >= K) & (lane < K + 3), total + pltpu.roll(total, 125, 1), total)
    return jnp.where(lane == row, out + total[:, K + 6 : K + 7], out)


def sum_parts(parts_ref):
    total = parts_ref[0].astype(jnp.float32)
    for part in range(1, parts_ref.shape[0]):
        total = total + parts_ref[part].astype(jnp.float32)
    return widen(total) if parts_ref.dtype == jnp.bfloat16 else total


def spread_kernel(parts_ref, out_ref):
    total = sum_parts(parts_ref)
    if out_ref.dtype == jnp.bfloat16:
        total = narrow(total)
    for copy in range(out_ref.shape[0]):
        out_ref[copy] = total


def spread_sum(parts, copies, dtype=jnp.float32):
    return pl.pallas_call(
        spread_kernel,
        out_shape=jax.ShapeDtypeStruct((copies, HALF, 128), dtype),
        in_specs=[VMEM],
        out_specs=VMEM,
        compiler_params=ROOM,
        name="spread_sum",
    )(parts)


def transform_kernel(parts_ref, weights_ref):
    folded = sum_parts(parts_ref)
    gram, projected = unfold(folded)
    row = lax.broadcasted_iota(jnp.int32, (K, K), 0)
    col = lax.broadcasted_iota(jnp.int32, (K, K), 1)
    eye = jnp.where(row == col, 1.0, 0.0).astype(jnp.float32)
    system = gram + (K - 1.0) * eye
    frob = jnp.sqrt(jnp.sum(system * system, keepdims=True))
    root = system / frob
    inverse = None
    for step in range(NS_ITERS):
        product = root if inverse is None else fine_dot(inverse, root)
        factor = 1.5 * eye - 0.5 * product
        if step < NS_ITERS - 1:
            root = fine_dot(root, factor)
        inverse = factor if inverse is None else fine_dot(factor, inverse)
    inverse_root = inverse / jnp.sqrt(frob)
    halfway = jnp.sum(inverse_root * projected, axis=0, keepdims=True)
    mean_shift = jnp.sum(inverse_root * halfway, axis=1, keepdims=True)
    weights_ref[...] = mean_shift + (K - 1.0) ** 0.5 * inverse_root


def transform(parts):
    return pl.pallas_call(
        transform_kernel,
        out_shape=jax.ShapeDtypeStruct((K, K), jnp.float32),
        in_specs=[VMEM],
        out_specs=VMEM,
        compiler_params=ROOM,
        cost_estimate=pl.CostEstimate(flops=COST, bytes_accessed=0, transcendentals=0),
        name="transform",
    )(parts)


def regroup(x, me, which):
    return jnp.concatenate(
        [x[pl.ds(pl.multiple_of(which(me, s) * MEMBERS, 8), MEMBERS), :] for s in range(GROUPS)], axis=0
    )


def coefficients(me, w_ref, turned):
    turned[...] = regroup(w_ref, me, group_from).T
    coeffs = regroup(turned, me, group_to).astype(jnp.bfloat16)
    return coeffs, 1.0 - jnp.sum(coeffs.astype(jnp.float32), axis=1, keepdims=True)


def mix(coeffs, keep, parts):
    stacked = jnp.concatenate([part.astype(jnp.float32) for part in parts], axis=0)
    center = jnp.sum(stacked, axis=0, keepdims=True) * (1.0 / K)
    mixed = jnp.dot(coeffs, stacked.astype(jnp.bfloat16), preferred_element_type=jnp.float32)
    return mixed + keep * center


def near_kernel(me_ref, w_ref, prior_ref, o1, o2, o3, b1, b2, b3, a0, a1, a2, a3, turned):
    coeffs, keep = coefficients(me_ref[0], w_ref, turned)
    cells = pl.ds(pl.multiple_of(me_ref[0] * TILE, TILE), TILE)
    for v in range(NEAR):
        parts = [ref[v] for ref in (o1, o2, o3)] if v < VOBS else [ref[v - VOBS] for ref in (b1, b2, b3)]
        parts = [prior_ref[v, :, cells]] + parts
        mixed = mix(coeffs, keep, parts)
        for g, out in enumerate((a0, a1, a2, a3)):
            out[v] = mixed[g * MEMBERS : (g + 1) * MEMBERS].astype(jnp.bfloat16)


def analyse_near(me, weights, prior, observed, bulk):
    return pl.pallas_call(
        near_kernel,
        out_shape=[jax.ShapeDtypeStruct((NEAR, MEMBERS, TILE), jnp.bfloat16)] * GROUPS,
        in_specs=[SMEM] + [VMEM] * 8,
        out_specs=[VMEM] * GROUPS,
        scratch_shapes=[pltpu.VMEM((K, K), jnp.float32)],
        compiler_params=ROOM,
        name="analyse_near",
    )(me, weights, prior, *observed, *bulk)


def far_kernel(me_ref, w_ref, near_ref, prior_ref, b1, b2, b3, out_ref, weights_ref, turned, result, sems):
    me = me_ref[0]
    cells = pl.ds(pl.multiple_of(me * TILE, TILE), TILE)
    copies = [
        pltpu.make_async_copy(near_ref, out_ref.at[pl.ds(0, NEAR), :, cells], sems.at[0]),
        pltpu.make_async_copy(w_ref, weights_ref, sems.at[1]),
    ]
    for copy in copies:
        copy.start()
    coeffs, keep = coefficients(me, w_ref, turned)
    for v in range(FAR):
        for c in range(GROUPS):
            lanes = pl.ds(c * TILE, TILE)
            parts = [prior_ref[NEAR + v, :, lanes]] + [ref[NEXT + c * FAR + v] for ref in (b1, b2, b3)]
            mixed = mix(coeffs[:MEMBERS], keep[:MEMBERS], parts)
            result[v, :, lanes] = mixed.astype(jnp.bfloat16)
        copies.append(pltpu.make_async_copy(result.at[v], out_ref.at[NEAR + v], sems.at[2 + v]))
        copies[-1].start()
    for copy in copies:
        copy.wait()


def analyse_far(me, weights, near, prior, bulk):
    return pl.pallas_call(
        far_kernel,
        out_shape=[
            jax.ShapeDtypeStruct((V, MEMBERS, GROUPS * TILE), jnp.bfloat16),
            jax.ShapeDtypeStruct((K, K), jnp.float32),
        ],
        in_specs=[SMEM] + [VMEM] * 6,
        out_specs=[ANY, ANY],
        scratch_shapes=[
            pltpu.VMEM((K, K), jnp.float32),
            pltpu.VMEM((FAR, MEMBERS, GROUPS * TILE), jnp.bfloat16),
            pltpu.SemaphoreType.DMA((2 + FAR,)),
        ],
        compiler_params=ROOM,
        name="analyse_far",
    )(me, weights, near, prior, *bulk)


def place_kernel(me_ref, c1, c2, c3, start_ref, out_ref, sems):
    del start_ref
    copies = []
    for s, chunk in enumerate((c1, c2, c3)):
        cells = pl.ds(pl.multiple_of(group_from(me_ref[0], s + 1) * TILE, TILE), TILE)
        copies.append(pltpu.make_async_copy(chunk, out_ref.at[pl.ds(0, NEAR), :, cells], sems.at[s]))
    for copy in copies:
        copy.start()
    for copy in copies:
        copy.wait()


def place(me, chunks, out):
    return pl.pallas_call(
        place_kernel,
        out_shape=jax.ShapeDtypeStruct(out.shape, out.dtype),
        in_specs=[SMEM] + [VMEM] * (GROUPS - 1) + [ANY],
        out_specs=ANY,
        scratch_shapes=[pltpu.SemaphoreType.DMA((GROUPS - 1,))],
        input_output_aliases={GROUPS: 0},
        compiler_params=ROOM,
        name="place",
    )(me, *chunks, out)


def ring(shift):
    return [(i, (i + shift) % GROUPS) for i in range(GROUPS)]


def scatter(chunks):
    return [lax.ppermute(chunk, "member", ring(s)) for s, chunk in enumerate(chunks, 1)]


def exchange(copies, axes):
    return lax.all_to_all(copies, axes, 0, 0, tiled=True)


def total(folded):
    copies = exchange(spread_sum(folded[None], PLANE, jnp.bfloat16), ("x", "z"))
    copies = exchange(spread_sum(copies, COLUMN, jnp.bfloat16), ("member", "core"))
    return copies


def body(prior, readings, error_spread, mapping, slots):
    member = lax.axis_index("member").astype(jnp.int32)
    always = member < GROUPS
    me = (member + 1 - always.astype(jnp.int32)).reshape(1)
    prior = jnp.transpose(prior, (1, 0, 2))
    packed = pack(me, prior)
    observed = scatter(packed[1:])
    bulk = scatter(pack_bulk(me, prior, packed[0]))
    folded = observe(
        me, jnp.transpose(slots, (1, 2, 0))[0], [packed[0]] + observed, mapping[:, 0], readings, error_spread
    )
    folded = lax.cond(
        always, total, lambda x: jnp.zeros((COLUMN, HALF, 128), jnp.bfloat16), folded
    )
    weights = transform(folded)
    near = analyse_near(me, weights, prior, observed, bulk)
    arrived = scatter(near[1:])
    out, weights = analyse_far(me, weights, near[0], prior, bulk)
    return (jnp.transpose(place(me, arrived, out), (1, 0, 2)), weights)


def solution(mesh):
    devices = mesh.devices.reshape(GROUPS, 4, 4, 2)
    axes = Mesh(devices, ("member", "x", "z", "core"))
    space = ("x", "z", "core")
    in_specs = (
        P("member", None, space),
        P(space, "member", None),
        P(space, "member", None),
        P(space, "member", None, None, None),
        P(space, "member", None),
    )
    out_specs = (P("member", None, space), P())
    return jax.shard_map(body, mesh=axes, in_specs=in_specs, out_specs=out_specs, check_vma=False)
```
